512 devices in a mesh: dp: 8 (over x, z_lo), dap: 64 (over y, z_hi, core).
Axes of the slice: x: 4, y: 8, z: 8 (z_hi: 4, z_lo: 2; z = z_hi * 2 + z_lo), core: 2. Of those that a mesh axis runs over, the one named last changes fastest.
Arguments:
- alignment_activations: bfloat16 [8, 512, 128, 256], P('dp', None, 'dap'), may hold values from -6 to 6
- upstream_adjoint: bfloat16 [8, 512, 128, 256], P('dp', 'dap'), may hold values from -6 to 6
- homolog_presence_flags: int32 [8, 512], P('dp'), may hold values from 0 to 1, as said below
- amino_presence_flags: int32 [8, 128], P('dp', 'dap'), may hold values from 0 to 1, as said below
- asking_projection_matrix: bfloat16 [256, 256], replicated, may hold values from -0.375 to 0.375
- lookup_projection_matrix: bfloat16 [256, 256], replicated, may hold values from -0.375 to 0.375
- content_projection_matrix: bfloat16 [256, 256], replicated, may hold values from -0.375 to 0.375
- sigmoid_projection_matrix: bfloat16 [256, 256], replicated, may hold values from -0.375 to 0.375
- sigmoid_offset_array: float32 [256], replicated, may hold values from -4 to 4
- emission_projection_matrix: bfloat16 [256, 256], replicated, may hold values from -0.375 to 0.375
- standardizer_multiplier: float32 [256], replicated, may hold values from 0.1 to 1.9
- standardizer_offset: float32 [256], replicated, may hold values from -3 to 3
Outputs:
- alignment_adjoint: bfloat16 [8, 512, 128, 256], P('dp', 'dap')
- grad_wquery: float32 [256, 256], replicated
- grad_wkey: float32 [256, 256], replicated
- grad_wvalue: float32 [256, 256], replicated
- grad_wgate: float32 [256, 256], replicated
- grad_wout: float32 [256, 256], replicated
- grad_vectors: float32 [4, 256], replicated
The draws below stay inside these ranges and needn't reach their ends.
Inputs may be any that keep to these rules, and one draw needn't show every extreme that they name: `homolog_presence_flags`: in each complex the real sequences form a prefix of 256 or more sequences. `amino_presence_flags`: in each complex the real residues form a prefix of 64 or more residues.
All inputs are finite; a program needn't handle non-finite values.
Results may differ from the reference program's by a relative error of at most 0.02.
Values may be sent and summed in bfloat16 or wider, within the bound.
No kernel may reach another device: no remote copies, remote signals or barrier semaphores. Data moves between devices by JAX's collectives and lax.ppermute only.
A program may use at most 64 MiB of HBM per device.

```python
import jax
import jax.numpy as jnp
from jax import lax

ALIGNMENT_DEPTH = 256
HEADS = 8
HOMOLOG_TOTAL = 512
ASSEMBLY_TOTAL = 8
AMINO_TOTAL = 128


def draw_homolog_presence_flags(key, part):
    key = jax.random.fold_in(key, 11)
    live = jax.random.randint(key, (ASSEMBLY_TOTAL, 1), HOMOLOG_TOTAL // 2, HOMOLOG_TOTAL + 1)
    return (jnp.arange(HOMOLOG_TOTAL)[None, :] < live).astype(jnp.int32)


def draw_amino_presence_flags(key, part):
    key = jax.random.fold_in(key, 23)
    live = jax.random.randint(key, (ASSEMBLY_TOTAL, 1), AMINO_TOTAL // 2, AMINO_TOTAL + 1)
    return (jnp.arange(AMINO_TOTAL)[None, :] < live).astype(jnp.int32)


def block_scale(rng, extent, pieces, low, high):
    factor_of, own = 1.0, jax.random.fold_in(rng, 6)
    for axis_at, parts in pieces:
        draws = jnp.exp(jax.random.uniform(jax.random.fold_in(own, axis_at), (parts,), jnp.float32, low / len(pieces), high / len(pieces)))
        factor_of = factor_of * jnp.repeat(draws, extent[axis_at] // parts).reshape([-1 if axis == axis_at else 1 for axis in range(len(extent))])
    return factor_of


def scatter_about(own_key, dims, scale, limit, pieces=(), dtype=jnp.bfloat16):
    level = block_scale(own_key, dims, pieces, -0.22, 0.18) if pieces else 1.0
    values = jax.random.normal(own_key, dims, jnp.float32) * scale * level
    return jnp.minimum(jnp.maximum(values, -limit), limit).astype(dtype)


def setup_inputs(seed: int = 0) -> dict:
    keys = jax.random.split(jax.random.key(seed), 13)
    alignment_activations = scatter_about(keys[0], (ASSEMBLY_TOTAL, HOMOLOG_TOTAL, AMINO_TOTAL, ALIGNMENT_DEPTH), 1.0, 6.0, ((0, 8), (2, 64)))
    upstream_adjoint = scatter_about(keys[1], (ASSEMBLY_TOTAL, HOMOLOG_TOTAL, AMINO_TOTAL, ALIGNMENT_DEPTH), 1.0, 6.0, ((0, 8), (1, 64)))
    homolog_presence_flags = draw_homolog_presence_flags(jax.random.fold_in(keys[12], 71), 0)
    amino_presence_flags = draw_amino_presence_flags(jax.random.fold_in(keys[12], 71), 0)
    asking_projection_matrix = scatter_about(keys[4], (ALIGNMENT_DEPTH, ALIGNMENT_DEPTH), ALIGNMENT_DEPTH ** -0.5, 0.375)
    lookup_projection_matrix = scatter_about(keys[5], (ALIGNMENT_DEPTH, ALIGNMENT_DEPTH), ALIGNMENT_DEPTH ** -0.5, 0.375)
    content_projection_matrix = scatter_about(keys[6], (ALIGNMENT_DEPTH, ALIGNMENT_DEPTH), ALIGNMENT_DEPTH ** -0.5, 0.375)
    sigmoid_projection_matrix = scatter_about(keys[7], (ALIGNMENT_DEPTH, ALIGNMENT_DEPTH), ALIGNMENT_DEPTH ** -0.5, 0.375)
    sigmoid_offset_array = scatter_about(keys[8], (ALIGNMENT_DEPTH,), 1.0, 4.0, (), jnp.float32)
    emission_projection_matrix = scatter_about(keys[9], (ALIGNMENT_DEPTH, ALIGNMENT_DEPTH), ALIGNMENT_DEPTH ** -0.5, 0.375)
    standardizer_multiplier = jnp.clip(1.0 + 0.18 * jax.random.normal(keys[10], (ALIGNMENT_DEPTH,), jnp.float32), 0.1, 1.9)
    standardizer_offset = scatter_about(keys[11], (ALIGNMENT_DEPTH,), 0.5, 3.0, (), jnp.float32)
    return {"alignment_activations": alignment_activations, "upstream_adjoint": upstream_adjoint, "homolog_presence_flags": homolog_presence_flags, "amino_presence_flags": amino_presence_flags, "asking_projection_matrix": asking_projection_matrix, "lookup_projection_matrix": lookup_projection_matrix, "content_projection_matrix": content_projection_matrix, "sigmoid_projection_matrix": sigmoid_projection_matrix, "sigmoid_offset_array": sigmoid_offset_array, "emission_projection_matrix": emission_projection_matrix, "standardizer_multiplier": standardizer_multiplier, "standardizer_offset": standardizer_offset}


EPS = 1e-05
MASKED = 1000000000.0

def product(form, left, right):
    return jnp.einsum(form, left.astype(jnp.float32), right.astype(jnp.float32))

def against(left, weight):
    return lax.dot_general(left, weight, (((1,), (1,)), ((), ())), preferred_element_type=jnp.float32)

def outer(left, right):
    return lax.dot_general(left, right, (((0,), (0,)), ((), ())), preferred_element_type=jnp.float32)

def standardize_lines(alignment_swapped):
    content_lines = alignment_swapped.astype(jnp.float32)
    centred = content_lines - lax.optimization_barrier(jnp.mean(content_lines, -1, keepdims=True))
    reciprocal_spread = lax.rsqrt(lax.optimization_barrier(jnp.mean(centred * centred, -1, keepdims=True)) + EPS)
    return (centred * reciprocal_spread, reciprocal_spread)

def split_heads(array, stack_members, homolog_lines, head_dim):
    return jnp.transpose(array.reshape(stack_members, homolog_lines, HEADS, head_dim), (0, 2, 1, 3)).reshape(stack_members * HEADS, homolog_lines, head_dim)

def join_heads(array, stack_members, homolog_lines, head_dim):
    return jnp.transpose(array.reshape(stack_members, HEADS, homolog_lines, head_dim), (0, 2, 1, 3)).reshape(stack_members * homolog_lines, HEADS * head_dim)

def attention_back(query, key_rows, value, gate, d_gated, key_bias, scale):
    scores = product('sd,td->st', query, key_rows) + key_bias[None, :]
    raised = jnp.exp(scores)
    probs = raised / lax.optimization_barrier(jnp.sum(raised, -1, keepdims=True))
    probs_b = probs.astype(jnp.bfloat16)
    attended = product('st,td->sd', probs_b, value)
    gated = (gate * attended).astype(jnp.bfloat16)
    d_attended = (d_gated * gate).astype(jnp.bfloat16)
    d_logit = (d_gated * attended * gate * (1.0 - gate)).astype(jnp.bfloat16)
    delta = lax.optimization_barrier(jnp.sum(d_attended.astype(jnp.float32) * attended, -1))
    d_probs = product('sd,td->st', d_attended, value)
    d_scores = (probs * (d_probs - delta[:, None])).astype(jnp.bfloat16)
    d_query = (product('st,td->sd', d_scores, key_rows) * scale).astype(jnp.bfloat16)
    d_key = product('st,sd->td', d_scores, query).astype(jnp.bfloat16)
    d_value = product('st,sd->td', probs_b, d_attended).astype(jnp.bfloat16)
    return (gated, d_logit, d_query, d_key, d_value)

def front_portion(alignment_swapped, upstream_adjoint_swapped, homolog_present, amino_present, asking_projection_matrix, lookup_projection_matrix, content_projection_matrix, sigmoid_projection_matrix, sigmoid_offset_array, emission_projection_matrix, standardizer_multiplier, standardizer_offset):
    stack_members, homolog_lines, feature_depth = alignment_swapped.shape
    head_dim = feature_depth // HEADS
    scale = head_dim ** (-0.5)
    standardized_estimate, reciprocal_spread = standardize_lines(alignment_swapped)
    flat = (standardized_estimate * standardizer_multiplier + standardizer_offset).astype(jnp.bfloat16).reshape(stack_members * homolog_lines, feature_depth)
    query = (jnp.dot(flat, asking_projection_matrix, preferred_element_type=jnp.float32) * scale).astype(jnp.bfloat16)
    key_rows = jnp.dot(flat, lookup_projection_matrix, preferred_element_type=jnp.float32).astype(jnp.bfloat16)
    value = jnp.dot(flat, content_projection_matrix, preferred_element_type=jnp.float32).astype(jnp.bfloat16)
    gate = jax.nn.sigmoid(jnp.dot(flat, sigmoid_projection_matrix, preferred_element_type=jnp.float32) + sigmoid_offset_array)
    d_update = upstream_adjoint_swapped * amino_present.astype(jnp.bfloat16)[:, None, None]
    d_flat = d_update.reshape(stack_members * homolog_lines, feature_depth)
    d_gated = against(d_flat, emission_projection_matrix)
    key_bias = (homolog_present.astype(jnp.float32) - 1.0) * MASKED
    items = tuple((split_heads(a, stack_members, homolog_lines, head_dim) for a in (query, key_rows, value, gate, d_gated)))
    results = lax.map(lambda item: attention_back(*item, key_bias, scale), items)
    gated, d_logit, d_query, d_key, d_value = (join_heads(a, stack_members, homolog_lines, head_dim) for a in results)
    opening_portion = jnp.concatenate([outer(gated, d_flat), outer(flat, d_logit), lax.optimization_barrier(jnp.sum(d_logit.astype(jnp.float32), 0))[None], lax.optimization_barrier(jnp.sum(d_flat.astype(jnp.float32), 0))[None]], 0)
    running_tally = (flat, standardized_estimate, reciprocal_spread, d_logit, d_query, d_key, d_value)
    return (running_tally, opening_portion)

def back_part(running_tally, asking_projection_matrix, lookup_projection_matrix, content_projection_matrix, sigmoid_projection_matrix, standardizer_multiplier):
    flat, standardized_estimate, reciprocal_spread, d_logit, d_query, d_key, d_value = running_tally
    d_normed = against(d_query, asking_projection_matrix) + against(d_key, lookup_projection_matrix) + against(d_value, content_projection_matrix) + against(d_logit, sigmoid_projection_matrix)
    d_normed = d_normed.reshape(standardized_estimate.shape)
    gain_grad = lax.optimization_barrier(jnp.sum(d_normed * standardized_estimate, (0, 1)))
    bias_grad = lax.optimization_barrier(jnp.sum(d_normed, (0, 1)))
    d_hat = d_normed * standardizer_multiplier
    d_branch = reciprocal_spread * (d_hat - lax.optimization_barrier(jnp.mean(d_hat, -1, keepdims=True)) - standardized_estimate * lax.optimization_barrier(jnp.mean(d_hat * standardized_estimate, -1, keepdims=True)))
    second = jnp.concatenate([outer(flat, d_query), outer(flat, d_key), outer(flat, d_value), gain_grad[None], bias_grad[None]], 0)
    return (d_branch, second)

def reference(alignment_activations, upstream_adjoint, homolog_presence_flags, amino_presence_flags, asking_projection_matrix, lookup_projection_matrix, content_projection_matrix, sigmoid_projection_matrix, sigmoid_offset_array, emission_projection_matrix, standardizer_multiplier, standardizer_offset):
    emitted_arrays = []
    opening_summation = jnp.zeros((2 * ALIGNMENT_DEPTH + 2, ALIGNMENT_DEPTH), jnp.float32)
    latter_summation = jnp.zeros((3 * ALIGNMENT_DEPTH + 2, ALIGNMENT_DEPTH), jnp.float32)
    for stack_position in range(ASSEMBLY_TOTAL):
        alignment_swapped = jnp.transpose(alignment_activations[stack_position], (1, 0, 2))
        upstream_adjoint_swapped = jnp.transpose(upstream_adjoint[stack_position], (1, 0, 2))
        running_tally, opening_portion = front_portion(alignment_swapped, upstream_adjoint_swapped, homolog_presence_flags[stack_position], amino_presence_flags[stack_position], asking_projection_matrix, lookup_projection_matrix, content_projection_matrix, sigmoid_projection_matrix, sigmoid_offset_array, emission_projection_matrix, standardizer_multiplier, standardizer_offset)
        d_branch, second = back_part(running_tally, asking_projection_matrix, lookup_projection_matrix, content_projection_matrix, sigmoid_projection_matrix, standardizer_multiplier)
        returned_answer = (upstream_adjoint_swapped.astype(jnp.float32) + d_branch).astype(jnp.bfloat16)
        emitted_arrays.append(jnp.transpose(returned_answer, (1, 0, 2)))
        opening_summation = opening_summation + opening_portion
        latter_summation = latter_summation + second
    scale_factor = (ASSEMBLY_TOTAL * HOMOLOG_TOTAL * AMINO_TOTAL) ** (-0.5)
    opening_summation = opening_summation * scale_factor
    latter_summation = latter_summation * scale_factor
    arrays_collected = jnp.stack([opening_summation[2 * ALIGNMENT_DEPTH], opening_summation[2 * ALIGNMENT_DEPTH + 1], latter_summation[3 * ALIGNMENT_DEPTH], latter_summation[3 * ALIGNMENT_DEPTH + 1]], 0)
    return (jnp.stack(emitted_arrays, 0), latter_summation[:ALIGNMENT_DEPTH], latter_summation[ALIGNMENT_DEPTH:2 * ALIGNMENT_DEPTH], latter_summation[2 * ALIGNMENT_DEPTH:3 * ALIGNMENT_DEPTH], opening_summation[ALIGNMENT_DEPTH:2 * ALIGNMENT_DEPTH], opening_summation[:ALIGNMENT_DEPTH], arrays_collected)
```

```python
import functools

import jax
import jax.numpy as jnp
from jax import lax
from jax.experimental import pallas as pl
from jax.experimental.pallas import tpu as pltpu
from jax.sharding import PartitionSpec as P

HEADS = 8
HEAD_DIM = 32
LANES = 128
PIECE = 48
EPS = 1e-05
MASKED = 1000000000.0
F32, BF16 = jnp.float32, jnp.bfloat16


def mm(left, right):
    return lax.dot_general(left, right, (((1,), (0,)), ((), ())), preferred_element_type=F32)


def against(left, weight):
    return lax.dot_general(left, weight, (((1,), (1,)), ((), ())), preferred_element_type=F32)


def row_sum(a):
    return jnp.sum(a, 0, keepdims=True)


def block_kernel(
    x_ref,
    up_ref,
    hom_ref,
    amino_ref,
    core_ref,
    wq_ref,
    wk_ref,
    wv_ref,
    wg_ref,
    bg_ref,
    wo_ref,
    gain_ref,
    off_ref,
    out_ref,
    keep_ref,
    send_ref,
    q_s,
    k_s,
    v_s,
    do_s,
    qt_s,
    dot_s,
    att_s,
    dq_s,
    dkt_s,
    dvt_s,
    gate_s,
    dg_s,
    out_s,
    grad_s,
    vec_s,
):
    members, lines, depth = x_ref.shape
    scale = HEAD_DIM**-0.5
    bias = (hom_ref[...].astype(F32) - 1.0) * MASKED
    lane_head = lax.broadcasted_iota(jnp.int32, (1, depth), 1) // HEAD_DIM
    vec_s[...] = jnp.zeros_like(vec_s)
    for r in range(members):
        x = x_ref[r].astype(F32)
        centred = x - jnp.mean(x, -1, keepdims=True)
        inv = lax.rsqrt(jnp.mean(centred * centred, -1, keepdims=True) + EPS)
        xhat = centred * inv
        normed = (xhat * gain_ref[...] + off_ref[...]).astype(BF16)
        query = (mm(normed, wq_ref[...]) * scale).astype(BF16)
        q_s[...] = query
        k_s[...] = mm(normed, wk_ref[...]).astype(BF16)
        v_s[...] = mm(normed, wv_ref[...]).astype(BF16)
        gate_s[...] = jax.nn.sigmoid(mm(normed, wg_ref[...]) + bg_ref[...])
        amino = amino_ref[0, r].astype(F32)
        up = up_ref[...].astype(F32)[:, 8 * r : 8 * r + 8, :].reshape(lines, depth)
        d_update = (up * amino).astype(BF16)
        dg_s[...] = against(d_update, wo_ref[...])
        d_att = (dg_s[...] * gate_s[...]).astype(BF16)
        do_s[...] = d_att
        qt_s[...] = query.T
        dot_s[...] = d_att.T
        att_s[...] = jnp.zeros_like(att_s)
        dq_s[...] = jnp.zeros_like(dq_s)

        def head(h, carry):
            own = (lane_head == h).astype(F32).astype(BF16)
            keys, values = k_s[...], v_s[...]
            q_h = q_s[...] * own
            do_h = do_s[...] * own
            rows = pl.ds(pl.multiple_of(h * HEAD_DIM, HEAD_DIM), HEAD_DIM)
            raised = jnp.exp(against(q_h, keys) + bias)
            probs = raised * (1.0 / jnp.sum(raised, -1, keepdims=True))
            probs_b = probs.astype(BF16)
            att = mm(probs_b, values * own)
            att_s[...] += att
            delta = jnp.sum(do_h.astype(F32) * att, -1, keepdims=True)
            d_scores = (probs * (against(do_h, values) - delta)).astype(BF16)
            dq_s[...] += mm(d_scores, keys * own)
            dkt_s[rows, :] = mm(qt_s[rows, :], d_scores).astype(BF16)
            dvt_s[rows, :] = mm(dot_s[rows, :], probs_b).astype(BF16)
            return carry

        lax.fori_loop(0, HEADS, head, 0, unroll=2)

        att, gate, d_gated = att_s[...], gate_s[...], dg_s[...]
        gated = (gate * att).astype(BF16)
        d_logit = (d_gated * att * gate * (1.0 - gate)).astype(BF16)
        dq = (dq_s[...] * scale).astype(BF16)
        dk = dkt_s[...].T
        dv = dvt_s[...].T
        d_normed = (
            against(dq, wq_ref[...])
            + against(dk, wk_ref[...])
            + against(dv, wv_ref[...])
            + against(d_logit, wg_ref[...])
        )
        d_hat = d_normed * gain_ref[...]
        d_branch = inv * (
            d_hat
            - jnp.mean(d_hat, -1, keepdims=True)
            - xhat * jnp.mean(d_hat * xhat, -1, keepdims=True)
        )
        out_s[:, 8 * r : 8 * r + 8, :] = (up + d_branch).reshape(lines // 8, 8, depth)
        normed_t = normed.T
        mats = (
            mm(normed_t, dq),
            mm(normed_t, dk),
            mm(normed_t, dv),
            mm(normed_t, d_logit),
            mm(gated.T, d_update),
        )
        vecs = (
            row_sum(d_logit.astype(F32)),
            row_sum(d_update.astype(F32)),
            row_sum(d_normed * xhat),
            row_sum(d_normed),
        )
        for i, g in enumerate(mats):
            grad_s[i] = g if r == 0 else grad_s[i] + g
        for i, g in enumerate(vecs):
            vec_s[i : i + 1, :] += g
    out_ref[...] = out_s[...].astype(BF16)
    low = core_ref[0] == 0
    pieces = []
    for half in range(2):
        lanes = slice(half * LANES, (half + 1) * LANES)
        parts = [grad_s[i][:, lanes].reshape(depth // 8, 8, LANES) for i in range(5)]
        parts.append(jnp.broadcast_to(vec_s[:, lanes][None], (depth // 8, 8, LANES)))
        pieces.append(jnp.concatenate(parts, 1))
    keep_ref[...] = jnp.where(low, pieces[0], pieces[1]).astype(BF16)
    send_ref[...] = jnp.where(low, pieces[1], pieces[0]).astype(BF16)


def block(x, up, hom, amino, core, wq, wk, wv, wg, bg, wo, gain, off):
    members, lines, depth = x.shape
    vm = pl.BlockSpec(memory_space=pltpu.VMEM)
    sm = pl.BlockSpec(memory_space=pltpu.SMEM)
    piece = jax.ShapeDtypeStruct((depth // 8, PIECE, LANES), BF16)
    tall, wide = (lines, depth), (depth, lines)
    pairs = members * HEADS
    return pl.pallas_call(
        block_kernel,
        out_shape=(jax.ShapeDtypeStruct(up.shape, BF16), piece, piece),
        in_specs=[vm, vm, vm, sm, sm] + [vm] * 8,
        out_specs=(vm, vm, vm),
        scratch_shapes=[pltpu.VMEM(tall, BF16)] * 4
        + [pltpu.VMEM(wide, BF16)] * 2
        + [pltpu.VMEM(tall, F32)] * 2
        + [pltpu.VMEM(wide, BF16)] * 2
        + [pltpu.VMEM(tall, F32)] * 2
        + [
            pltpu.VMEM(up.shape, F32),
            pltpu.VMEM((5, depth, depth), F32),
            pltpu.VMEM((8, depth), F32),
        ],
        compiler_params=pltpu.CompilerParams(vmem_limit_bytes=48 << 20),
        cost_estimate=pl.CostEstimate(
            flops=pairs * 12 * lines * lines * HEAD_DIM,
            bytes_accessed=4 << 20,
            transcendentals=pairs * lines * lines,
        ),
        name="attention_block",
    )(x, up, hom, amino, core, wq, wk, wv, wg, bg, wo, gain, off)


def unpack_kernel(factor, core_ref, own_ref, other_ref, *out_refs):
    low = core_ref[0] == 0
    for half in range(2):
        lanes = slice(half * LANES, (half + 1) * LANES)
        first = low if half == 0 else jnp.logical_not(low)
        own = own_ref[...].astype(F32)
        other = other_ref[...].astype(F32)
        g = jnp.where(first, own, other) * factor
        depth = out_refs[0].shape[0]
        for i in range(5):
            out_refs[i][:, lanes] = g[:, 8 * i : 8 * i + 8, :].reshape(depth, LANES)
        out_refs[5][:, lanes] = g[0, 40:44, :]


def unpack(core, own, other, depth, factor):
    vm = pl.BlockSpec(memory_space=pltpu.VMEM)
    sm = pl.BlockSpec(memory_space=pltpu.SMEM)
    return pl.pallas_call(
        functools.partial(unpack_kernel, factor),
        out_shape=(jax.ShapeDtypeStruct((depth, depth), F32),) * 5
        + (jax.ShapeDtypeStruct((4, depth), F32),),
        in_specs=[sm, vm, vm],
        out_specs=(vm,) * 6,
        compiler_params=pltpu.CompilerParams(vmem_limit_bytes=32 << 20),
        name="unpack",
    )(core, own, other)


def exchange(a, axis, groups=None):
    return lax.all_to_all(
        a, axis, split_axis=0, concat_axis=0, tiled=True, axis_index_groups=groups
    )


def merge_kernel(parts_ref, out_ref):
    total = jnp.sum(parts_ref[...].astype(F32), 0, keepdims=True)
    out_ref[...] = jnp.broadcast_to(total, out_ref.shape).astype(BF16)


def merge(parts, copies):
    vm = pl.BlockSpec(memory_space=pltpu.VMEM)
    return pl.pallas_call(
        merge_kernel,
        out_shape=jax.ShapeDtypeStruct((copies,) + parts.shape[1:], BF16),
        in_specs=[vm],
        out_specs=vm,
        compiler_params=pltpu.CompilerParams(vmem_limit_bytes=16 << 20),
        name="merge",
    )(parts)


def shards(x, up, hom, amino, wq, wk, wv, wg, bg, wo, gain, off):
    _, near, residues, depth = up.shape
    n_dp, n_dap = lax.axis_size("dp"), lax.axis_size("dap")
    lines, members = x.shape[1], x.shape[2]
    chips = n_dap // 2
    partner = [(i, i ^ 1) for i in range(n_dap)]
    same_core = [[2 * i + c for i in range(chips)] for c in range(2)]
    core = (lax.axis_index("dap") % 2).astype(jnp.int32).reshape(1)

    rows = jnp.transpose(up[0].reshape(near, n_dap, members, depth), (1, 2, 0, 3))
    local_up = exchange(rows.reshape(n_dap, members * near, depth), "dap")
    swapped = jnp.transpose(x[0], (1, 0, 2))
    out, keep, send = block(
        swapped, local_up, hom, amino, core, wq, wk, wv, wg, bg[None], wo, gain[None], off[None]
    )

    got = lax.ppermute(send, "dap", partner)
    half = (keep.astype(F32) + got.astype(F32)).astype(BF16)
    parts = exchange(half, "dap", same_core)
    parts = exchange(merge(parts, n_dp), "dp")
    pieces = merge(parts, chips)
    own = exchange(pieces, "dap", same_core)
    other = lax.ppermute(own, "dap", partner)
    factor = float((n_dp * lines * residues) ** (-0.5))
    grads = unpack(core, own, other, depth, factor)

    back = exchange(out, "dap").reshape(n_dap, members, near, depth)
    adjoint = jnp.transpose(back, (2, 0, 1, 3)).reshape(1, near, residues, depth)
    return (adjoint,) + tuple(grads)


def solution(mesh):
    in_specs = (
        P("dp", None, "dap", None),
        P("dp", "dap", None, None),
        P("dp", None),
        P("dp", "dap"),
    ) + (P(),) * 8
    out_specs = (P("dp", "dap", None, None),) + (P(),) * 6
    return jax.shard_map(shards, mesh=mesh, in_specs=in_specs, out_specs=out_specs, check_vma=False)
```

```python
import functools

import jax
import jax.numpy as jnp
from jax import lax
from jax.experimental import pallas as pl
from jax.experimental.pallas import tpu as pltpu
from jax.sharding import PartitionSpec as P

HEADS = 8
HEAD_DIM = 32
LANES = 128
PIECE = 48
MSA = 32
EPS = 1e-05
MASKED = 1000000000.0
F32, BF16 = jnp.float32, jnp.bfloat16


def mm(left, right):
    return lax.dot_general(left, right, (((1,), (0,)), ((), ())), preferred_element_type=F32)


def against(left, weight):
    return lax.dot_general(left, weight, (((1,), (1,)), ((), ())), preferred_element_type=F32)


def row_sum(a):
    return jnp.sum(a, 0, keepdims=True)


def front_kernel(
    x_ref,
    hom_ref,
    wq_ref,
    wk_ref,
    wv_ref,
    wg_ref,
    bg_ref,
    gain_ref,
    off_ref,
    xhat_ref,
    inv_ref,
    nt_ref,
    k_ref,
    v_ref,
    qt_ref,
    gate_ref,
    att_ref,
    probs_ref,
    q_s,
):
    members, lines, depth = x_ref.shape
    bias = (hom_ref[...].astype(F32) - 1.0) * MASKED
    lane_head = lax.broadcasted_iota(jnp.int32, (1, depth), 1) // HEAD_DIM
    for r in range(members):
        x = x_ref[r].astype(F32)
        centred = x - jnp.mean(x, -1, keepdims=True)
        inv = lax.rsqrt(jnp.mean(centred * centred, -1, keepdims=True) + EPS)
        xhat = centred * inv
        xhat_ref[r] = xhat
        inv_ref[r] = jnp.broadcast_to(inv, (lines, LANES))
        normed = (xhat * gain_ref[...] + off_ref[...]).astype(BF16)
        nt_ref[r] = normed.T
        query = (mm(normed, wq_ref[...]) * HEAD_DIM**-0.5).astype(BF16)
        q_s[...] = query
        qt_ref[r] = query.T
        k_ref[r] = mm(normed, wk_ref[...]).astype(BF16)
        v_ref[r] = mm(normed, wv_ref[...]).astype(BF16)
        gate_ref[r] = jax.nn.sigmoid(mm(normed, wg_ref[...]) + bg_ref[...])
        att_ref[r] = jnp.zeros((lines, depth), F32)

        def head(h, carry):
            own = (lane_head == h).astype(F32).astype(BF16)
            raised = jnp.exp(against(q_s[...] * own, k_ref[r]) + bias)
            probs = raised * (1.0 / jnp.sum(raised, -1, keepdims=True))
            probs_b = probs.astype(BF16)
            probs_ref[r, h] = probs_b
            att_ref[r] += mm(probs_b, v_ref[r] * own)
            return carry

        lax.fori_loop(0, HEADS, head, 0, unroll=2)


def back_kernel(
    up_ref,
    amino_ref,
    core_ref,
    xhat_ref,
    inv_ref,
    nt_ref,
    k_ref,
    v_ref,
    qt_ref,
    gate_ref,
    att_ref,
    probs_ref,
    wq_ref,
    wk_ref,
    wv_ref,
    wg_ref,
    wo_ref,
    gain_ref,
    keep_ref,
    send_ref,
    do_s,
    dot_s,
    prod_s,
    dg_s,
    dq_s,
    dkt_s,
    dvt_s,
    out_s,
    grad_s,
    vec_s,
):
    members, lines, depth = xhat_ref.shape
    lane_head = lax.broadcasted_iota(jnp.int32, (1, depth), 1) // HEAD_DIM
    vec_s[...] = jnp.zeros_like(vec_s)
    for r in range(members):
        amino = amino_ref[0, r].astype(F32)
        up = up_ref[...].astype(F32)[:, 8 * r : 8 * r + 8, :].reshape(lines, depth)
        d_update = (up * amino).astype(BF16)
        dg_s[...] = against(d_update, wo_ref[...])
        d_att = (dg_s[...] * gate_ref[r]).astype(BF16)
        do_s[...] = d_att
        dot_s[...] = d_att.T
        prod_s[...] = d_att.astype(F32) * att_ref[r]
        dq_s[...] = jnp.zeros_like(dq_s)

        def head(h, carry):
            mask = (lane_head == h).astype(F32)
            own = mask.astype(BF16)
            rows = pl.ds(pl.multiple_of(h * HEAD_DIM, HEAD_DIM), HEAD_DIM)
            probs_b = probs_ref[r, h]
            delta = jnp.sum(prod_s[...] * mask, -1, keepdims=True)
            d_probs = against(do_s[...] * own, v_ref[r])
            d_scores = (probs_b.astype(F32) * (d_probs - delta)).astype(BF16)
            dq_s[...] += mm(d_scores, k_ref[r] * own)
            dkt_s[rows, :] = mm(qt_ref[r, rows, :], d_scores).astype(BF16)
            dvt_s[rows, :] = mm(dot_s[rows, :], probs_b).astype(BF16)
            return carry

        lax.fori_loop(0, HEADS, head, 0, unroll=2)

        att, gate, d_gated, xhat = att_ref[r], gate_ref[r], dg_s[...], xhat_ref[r]
        gated = (gate * att).astype(BF16)
        d_logit = (d_gated * att * gate * (1.0 - gate)).astype(BF16)
        dq = (dq_s[...] * HEAD_DIM**-0.5).astype(BF16)
        dk = dkt_s[...].T
        dv = dvt_s[...].T
        d_normed = (
            against(dq, wq_ref[...])
            + against(dk, wk_ref[...])
            + against(dv, wv_ref[...])
            + against(d_logit, wg_ref[...])
        )
        d_hat = d_normed * gain_ref[...]
        d_branch = inv_ref[r][:, :1] * (
            d_hat
            - jnp.mean(d_hat, -1, keepdims=True)
            - xhat * jnp.mean(d_hat * xhat, -1, keepdims=True)
        )
        out_s[:, 8 * r : 8 * r + 8, :] = (up + d_branch).reshape(lines // 8, 8, depth)
        normed_t = nt_ref[r]
        mats = (
            mm(normed_t, dq),
            mm(normed_t, dk),
            mm(normed_t, dv),
            mm(normed_t, d_logit),
            mm(gated.T, d_update),
        )
        vecs = (
            row_sum(d_logit.astype(F32)),
            row_sum(d_update.astype(F32)),
            row_sum(d_normed * xhat),
            row_sum(d_normed),
        )
        for i, g in enumerate(mats):
            grad_s[i] = g if r == 0 else grad_s[i] + g
        for i, g in enumerate(vecs):
            vec_s[i : i + 1, :] += g
    low = core_ref[0] == 0
    chips = depth // 8
    pairs = out_s[...].reshape(chips, 2, 16, depth)
    for half in range(2):
        lanes = slice(half * LANES, (half + 1) * LANES)
        rows = slice(16 * half, 16 * half + 16)
        zero, one = pairs[:, 0, :, lanes], pairs[:, 1, :, lanes]
        keep_ref[:, rows, :] = jnp.where(low, zero, one).astype(BF16)
        send_ref[:, rows, :] = jnp.where(low, one, zero).astype(BF16)
    pieces = []
    for half in range(2):
        lanes = slice(half * LANES, (half + 1) * LANES)
        parts = [grad_s[i][:, lanes].reshape(chips, 8, LANES) for i in range(5)]
        parts.append(jnp.broadcast_to(vec_s[:, lanes][None], (chips, 8, LANES)))
        pieces.append(jnp.concatenate(parts, 1))
    keep_ref[:, MSA:, :] = jnp.where(low, pieces[0], pieces[1]).astype(BF16)
    send_ref[:, MSA:, :] = jnp.where(low, pieces[1], pieces[0]).astype(BF16)


def specs(n):
    return [pl.BlockSpec(memory_space=pltpu.VMEM)] * n


SMEM = pl.BlockSpec(memory_space=pltpu.SMEM)


def shape(dims, dtype):
    return jax.ShapeDtypeStruct(dims, dtype)


def front(x, hom, wq, wk, wv, wg, bg, gain, off):
    members, lines, depth = x.shape
    tall, wide = (members, lines, depth), (members, depth, lines)
    pairs = members * HEADS
    return pl.pallas_call(
        front_kernel,
        out_shape=(
            shape(tall, F32),
            shape((members, lines, LANES), F32),
            shape(wide, BF16),
            shape(tall, BF16),
            shape(tall, BF16),
            shape(wide, BF16),
            shape(tall, F32),
            shape(tall, F32),
            shape((members, HEADS, lines, lines), BF16),
        ),
        in_specs=specs(9),
        out_specs=specs(9),
        scratch_shapes=[pltpu.VMEM((lines, depth), BF16)],
        compiler_params=pltpu.CompilerParams(vmem_limit_bytes=28 << 20),
        cost_estimate=pl.CostEstimate(
            flops=pairs * 32 * lines * lines * HEAD_DIM,
            bytes_accessed=4 << 20,
            transcendentals=pairs * lines * lines,
        ),
        name="attention_front",
    )(x, hom, wq, wk, wv, wg, bg, gain, off)


def back(up, amino, core, saved, wq, wk, wv, wg, wo, gain):
    members, lines, depth = saved[0].shape
    tall, wide = (lines, depth), (depth, lines)
    pairs = members * HEADS
    parcel = shape((depth // 8, MSA + PIECE, LANES), BF16)
    return pl.pallas_call(
        back_kernel,
        out_shape=(parcel, parcel),
        in_specs=specs(1) + [SMEM, SMEM] + specs(15),
        out_specs=specs(2),
        scratch_shapes=[
            pltpu.VMEM(tall, BF16),
            pltpu.VMEM(wide, BF16),
            pltpu.VMEM(tall, F32),
            pltpu.VMEM(tall, F32),
            pltpu.VMEM(tall, F32),
            pltpu.VMEM(wide, BF16),
            pltpu.VMEM(wide, BF16),
            pltpu.VMEM(up.shape, F32),
            pltpu.VMEM((5, depth, depth), F32),
            pltpu.VMEM((8, depth), F32),
        ],
        compiler_params=pltpu.CompilerParams(vmem_limit_bytes=36 << 20),
        cost_estimate=pl.CostEstimate(
            flops=pairs * 64 * lines * lines * HEAD_DIM,
            bytes_accessed=4 << 20,
            transcendentals=0,
        ),
        name="attention_back",
    )(up, amino, core, *saved, wq, wk, wv, wg, wo, gain)


def combine_kernel(core_ref, keep_ref, got_ref, ride_ref):
    low = core_ref[0] == 0
    for half in range(2):
        rows = slice(16 * half, 16 * half + 16)
        keep, got = keep_ref[:, rows, :], got_ref[:, rows, :]
        at = 32 * half
        ride_ref[:, at : at + 16, :] = jnp.where(low, keep, got)
        ride_ref[:, at + 16 : at + 32, :] = jnp.where(low, got, keep)
    total = keep_ref[:, MSA:, :].astype(F32) + got_ref[:, MSA:, :].astype(F32)
    ride_ref[:, 2 * MSA :, :] = total.astype(BF16)


def combine(core, keep, got):
    return pl.pallas_call(
        combine_kernel,
        out_shape=shape((keep.shape[0], 2 * MSA + PIECE, LANES), BF16),
        in_specs=[SMEM] + specs(2),
        out_specs=specs(1)[0],
        compiler_params=pltpu.CompilerParams(vmem_limit_bytes=16 << 20),
        name="combine",
    )(core, keep, got)


def merge_kernel(parts_ref, out_ref):
    start = parts_ref.shape[1] - PIECE
    total = jnp.sum(parts_ref[:, start:, :].astype(F32), 0, keepdims=True)
    out_ref[...] = jnp.broadcast_to(total, out_ref.shape).astype(BF16)


def merge(parts, copies):
    return pl.pallas_call(
        merge_kernel,
        out_shape=shape((copies, PIECE, LANES), BF16),
        in_specs=specs(1),
        out_specs=specs(1)[0],
        compiler_params=pltpu.CompilerParams(vmem_limit_bytes=16 << 20),
        name="merge",
    )(parts)


def unpack_kernel(factor, core_ref, own_ref, other_ref, *out_refs):
    low = core_ref[0] == 0
    for half in range(2):
        lanes = slice(half * LANES, (half + 1) * LANES)
        first = low if half == 0 else jnp.logical_not(low)
        own = own_ref[...].astype(F32)
        other = other_ref[...].astype(F32)
        g = jnp.where(first, own, other) * factor
        depth = out_refs[0].shape[0]
        for i in range(5):
            out_refs[i][:, lanes] = g[:, 8 * i : 8 * i + 8, :].reshape(depth, LANES)
        out_refs[5][:, lanes] = g[0, 40:44, :]


def unpack(core, own, other, depth, factor):
    vm = pl.BlockSpec(memory_space=pltpu.VMEM)
    sm = pl.BlockSpec(memory_space=pltpu.SMEM)
    return pl.pallas_call(
        functools.partial(unpack_kernel, factor),
        out_shape=(jax.ShapeDtypeStruct((depth, depth), F32),) * 5
        + (jax.ShapeDtypeStruct((4, depth), F32),),
        in_specs=[sm, vm, vm],
        out_specs=(vm,) * 6,
        compiler_params=pltpu.CompilerParams(vmem_limit_bytes=32 << 20),
        name="unpack",
    )(core, own, other)


def exchange(a, axis, groups=None):
    return lax.all_to_all(
        a, axis, split_axis=0, concat_axis=0, tiled=True, axis_index_groups=groups
    )


def shards(x, up, hom, amino, wq, wk, wv, wg, bg, wo, gain, off):
    _, near, residues, depth = up.shape
    n_dp, n_dap = lax.axis_size("dp"), lax.axis_size("dap")
    lines, members = x.shape[1], x.shape[2]
    chips = n_dap // 2
    partner = [(i, i ^ 1) for i in range(n_dap)]
    same_core = [[2 * i + c for i in range(chips)] for c in range(2)]
    core = (lax.axis_index("dap") % 2).astype(jnp.int32).reshape(1)

    rows = jnp.transpose(up[0].reshape(near, n_dap, members, depth), (1, 2, 0, 3))
    local_up = exchange(rows.reshape(n_dap, members * near, depth), "dap")
    swapped = jnp.transpose(x[0], (1, 0, 2))
    gain, off, bg = gain[None], off[None], bg[None]
    saved = front(swapped, hom, wq, wk, wv, wg, bg, gain, off)
    keep, send = back(local_up, amino, core, saved, wq, wk, wv, wg, wo, gain)

    got = lax.ppermute(send, "dap", partner)
    parts = exchange(combine(core, keep, got), "dap", same_core)
    pieces = exchange(merge(parts, n_dp), "dp")
    own = exchange(merge(pieces, chips), "dap", same_core)
    other = lax.ppermute(own, "dap", partner)
    factor = float((n_dp * lines * residues) ** (-0.5))
    grads = unpack(core, own, other, depth, factor)

    msa = parts[:, : 2 * MSA].reshape(chips, depth // LANES, 2, members, near, LANES)
    adjoint = jnp.transpose(msa, (4, 0, 2, 3, 1, 5)).reshape(1, near, residues, depth)
    return (adjoint,) + tuple(grads)


def solution(mesh):
    in_specs = (
        P("dp", None, "dap", None),
        P("dp", "dap", None, None),
        P("dp", None),
        P("dp", "dap"),
    ) + (P(),) * 8
    out_specs = (P("dp", "dap", None, None),) + (P(),) * 6
    return jax.shard_map(shards, mesh=mesh, in_specs=in_specs, out_specs=out_specs, check_vma=False)
```

```python
import functools

import jax
import jax.numpy as jnp
from jax import lax
from jax.experimental import pallas as pl
from jax.experimental.pallas import tpu as pltpu
from jax.sharding import PartitionSpec as P

HEADS = 8
HEAD_DIM = 32
LANES = 128
PIECE = 48
MSA = 32
GROUP = 8
VMEM_BYTES = 60 << 20
EPS = 1e-05
MASKED = 1000000000.0
F32, BF16 = jnp.float32, jnp.bfloat16


def mm(left, right):
    return lax.dot_general(left, right, (((1,), (0,)), ((), ())), preferred_element_type=F32)


def against(left, weight):
    return lax.dot_general(left, weight, (((1,), (1,)), ((), ())), preferred_element_type=F32)


def row_sum(a):
    return jnp.sum(a, 0, keepdims=True)


def front_kernel(
    x_ref,
    hom_ref,
    wq_ref,
    wk_ref,
    wv_ref,
    wg_ref,
    bg_ref,
    gain_ref,
    off_ref,
    xhat_ref,
    inv_ref,
    nt_ref,
    k_ref,
    v_ref,
    qt_ref,
    gate_ref,
    att_ref,
    probs_ref,
    q_s,
):
    _, lines, depth = x_ref.shape
    group = probs_ref.shape[1]
    step = pl.program_id(1)
    bias = (hom_ref[...].astype(F32) - 1.0) * MASKED
    lane_head = lax.broadcasted_iota(jnp.int32, (1, depth), 1) // HEAD_DIM

    @pl.when(step == 0)
    def _():
        x = x_ref[0].astype(F32)
        centred = x - jnp.mean(x, -1, keepdims=True)
        inv = lax.rsqrt(jnp.mean(centred * centred, -1, keepdims=True) + EPS)
        xhat = centred * inv
        xhat_ref[0] = xhat
        inv_ref[0] = jnp.broadcast_to(inv, (lines, LANES))
        normed = (xhat * gain_ref[...] + off_ref[...]).astype(BF16)
        nt_ref[0] = normed.T
        query = (mm(normed, wq_ref[...]) * HEAD_DIM**-0.5).astype(BF16)
        q_s[...] = query
        qt_ref[0] = query.T
        k_ref[0] = mm(normed, wk_ref[...]).astype(BF16)
        v_ref[0] = mm(normed, wv_ref[...]).astype(BF16)
        gate_ref[0] = jax.nn.sigmoid(mm(normed, wg_ref[...]) + bg_ref[...])
        att_ref[0] = jnp.zeros((lines, depth), F32)

    for j in range(group):
        own = (lane_head == step * group + j).astype(F32).astype(BF16)
        raised = jnp.exp(against(q_s[...] * own, k_ref[0]) + bias)
        probs = raised * (1.0 / jnp.sum(raised, -1, keepdims=True))
        probs_b = probs.astype(BF16)
        probs_ref[0, j] = probs_b
        att_ref[0] += mm(probs_b, v_ref[0] * own)


def back_kernel(
    up_ref,
    amino_ref,
    core_ref,
    xhat_ref,
    inv_ref,
    nt_ref,
    k_ref,
    v_ref,
    qt_ref,
    gate_ref,
    att_ref,
    probs_ref,
    wq_ref,
    wk_ref,
    wv_ref,
    wg_ref,
    wo_ref,
    gain_ref,
    keep_ref,
    send_ref,
    up_s,
    do_s,
    dot_s,
    prod_s,
    dg_s,
    dq_s,
    dkt_s,
    dvt_s,
    out_s,
    grad_s,
    vec_s,
):
    members, lines, depth = up_s.shape
    group = probs_ref.shape[1]
    r, step = pl.program_id(0), pl.program_id(1)
    last = pl.num_programs(1) - 1
    lane_head = lax.broadcasted_iota(jnp.int32, (1, depth), 1) // HEAD_DIM

    def update():
        return (up_s[r] * amino_ref[0, r].astype(F32)).astype(BF16)

    @pl.when(jnp.logical_and(r == 0, step == 0))
    def _():
        up = up_ref[...].astype(F32)
        for i in range(members):
            up_s[i] = up[:, 8 * i : 8 * i + 8, :].reshape(lines, depth)
        grad_s[...] = jnp.zeros_like(grad_s)
        vec_s[...] = jnp.zeros_like(vec_s)

    @pl.when(step == 0)
    def _():
        dg_s[...] = against(update(), wo_ref[...])
        d_att = (dg_s[...] * gate_ref[0]).astype(BF16)
        do_s[...] = d_att
        dot_s[...] = d_att.T
        prod_s[...] = d_att.astype(F32) * att_ref[0]
        dq_s[...] = jnp.zeros_like(dq_s)

    for j in range(group):
        h = step * group + j
        mask = (lane_head == h).astype(F32)
        own = mask.astype(BF16)
        rows = pl.ds(pl.multiple_of(h * HEAD_DIM, HEAD_DIM), HEAD_DIM)
        probs_b = probs_ref[0, j]
        delta = jnp.sum(prod_s[...] * mask, -1, keepdims=True)
        d_probs = against(do_s[...] * own, v_ref[0])
        d_scores = (probs_b.astype(F32) * (d_probs - delta)).astype(BF16)
        dq_s[...] += mm(d_scores, k_ref[0] * own)
        dkt_s[rows, :] = mm(qt_ref[0, rows, :], d_scores).astype(BF16)
        dvt_s[rows, :] = mm(dot_s[rows, :], probs_b).astype(BF16)

    @pl.when(step == last)
    def _():
        att, gate, d_gated, xhat = att_ref[0], gate_ref[0], dg_s[...], xhat_ref[0]
        d_update = update()
        gated = (gate * att).astype(BF16)
        d_logit = (d_gated * att * gate * (1.0 - gate)).astype(BF16)
        dq = (dq_s[...] * HEAD_DIM**-0.5).astype(BF16)
        dk = dkt_s[...].T
        dv = dvt_s[...].T
        d_normed = (
            against(dq, wq_ref[...])
            + against(dk, wk_ref[...])
            + against(dv, wv_ref[...])
            + against(d_logit, wg_ref[...])
        )
        d_hat = d_normed * gain_ref[...]
        d_branch = inv_ref[0][:, :1] * (
            d_hat
            - jnp.mean(d_hat, -1, keepdims=True)
            - xhat * jnp.mean(d_hat * xhat, -1, keepdims=True)
        )
        out_s[r] = (up_s[r] + d_branch).reshape(lines // 8, 8, depth)
        normed_t = nt_ref[0]
        mats = (
            mm(normed_t, dq),
            mm(normed_t, dk),
            mm(normed_t, dv),
            mm(normed_t, d_logit),
            mm(gated.T, d_update),
        )
        vecs = (
            row_sum(d_logit.astype(F32)),
            row_sum(d_update.astype(F32)),
            row_sum(d_normed * xhat),
            row_sum(d_normed),
        )
        for i, g in enumerate(mats):
            grad_s[i] += g
        for i, g in enumerate(vecs):
            vec_s[i : i + 1, :] += g

    @pl.when(jnp.logical_and(r == members - 1, step == last))
    def _():
        low = core_ref[0] == 0
        chips = depth // 8
        pairs = jnp.concatenate([out_s[i] for i in range(members)], 1)
        pairs = pairs.reshape(chips, 2, 8 * members, depth)
        for half in range(2):
            lanes = slice(half * LANES, (half + 1) * LANES)
            rows = slice(16 * half, 16 * half + 16)
            zero, one = pairs[:, 0, :, lanes], pairs[:, 1, :, lanes]
            keep_ref[:, rows, :] = jnp.where(low, zero, one).astype(BF16)
            send_ref[:, rows, :] = jnp.where(low, one, zero).astype(BF16)
        pieces = []
        for half in range(2):
            lanes = slice(half * LANES, (half + 1) * LANES)
            parts = [grad_s[i][:, lanes].reshape(chips, 8, LANES) for i in range(5)]
            parts.append(jnp.broadcast_to(vec_s[:, lanes][None], (chips, 8, LANES)))
            pieces.append(jnp.concatenate(parts, 1))
        keep_ref[:, MSA:, :] = jnp.where(low, pieces[0], pieces[1]).astype(BF16)
        send_ref[:, MSA:, :] = jnp.where(low, pieces[1], pieces[0]).astype(BF16)


def specs(n):
    return [pl.BlockSpec(memory_space=pltpu.VMEM)] * n


SMEM = pl.BlockSpec(memory_space=pltpu.SMEM)


def shape(dims, dtype):
    return jax.ShapeDtypeStruct(dims, dtype)


def whole(a):
    return pl.BlockSpec(a.shape, lambda r, h: (0,) * len(a.shape))


def by_member(a):
    return pl.BlockSpec((1,) + a.shape[1:], lambda r, h: (r,) + (0,) * (len(a.shape) - 1))


def by_group(a):
    return pl.BlockSpec((1, GROUP) + a.shape[2:], lambda r, h: (r, h, 0, 0))


def front(x, hom, wq, wk, wv, wg, bg, gain, off):
    members, lines, depth = x.shape
    tall, wide = (members, lines, depth), (members, depth, lines)
    pairs = members * HEADS
    outs = (
        shape(tall, F32),
        shape((members, lines, LANES), F32),
        shape(wide, BF16),
        shape(tall, BF16),
        shape(tall, BF16),
        shape(wide, BF16),
        shape(tall, F32),
        shape(tall, F32),
        shape((members, HEADS, lines, lines), BF16),
    )
    return pl.pallas_call(
        front_kernel,
        grid=(members, HEADS // GROUP),
        out_shape=outs,
        in_specs=[by_member(x)] + [whole(a) for a in (hom, wq, wk, wv, wg, bg, gain, off)],
        out_specs=[by_member(a) for a in outs[:-1]] + [by_group(outs[-1])],
        scratch_shapes=[pltpu.VMEM((lines, depth), BF16)],
        compiler_params=pltpu.CompilerParams(vmem_limit_bytes=VMEM_BYTES),
        cost_estimate=pl.CostEstimate(
            flops=pairs * 32 * lines * lines * HEAD_DIM,
            bytes_accessed=14 << 20,
            transcendentals=pairs * lines * lines,
        ),
        name="attention_front",
    )(x, hom, wq, wk, wv, wg, bg, gain, off)


def back(up, amino, core, saved, wq, wk, wv, wg, wo, gain):
    members, lines, depth = saved[0].shape
    tall, wide = (lines, depth), (depth, lines)
    pairs = members * HEADS
    parcel = shape((depth // 8, MSA + PIECE, LANES), BF16)
    return pl.pallas_call(
        back_kernel,
        grid=(members, HEADS // GROUP),
        out_shape=(parcel, parcel),
        in_specs=[whole(up), SMEM, SMEM]
        + [by_member(a) for a in saved[:-1]]
        + [by_group(saved[-1])]
        + [whole(a) for a in (wq, wk, wv, wg, wo, gain)],
        out_specs=[whole(parcel), whole(parcel)],
        scratch_shapes=[
            pltpu.VMEM((members,) + tall, F32),
            pltpu.VMEM(tall, BF16),
            pltpu.VMEM(wide, BF16),
            pltpu.VMEM(tall, F32),
            pltpu.VMEM(tall, F32),
            pltpu.VMEM(tall, F32),
            pltpu.VMEM(wide, BF16),
            pltpu.VMEM(wide, BF16),
            pltpu.VMEM((members, lines // 8, 8, depth), F32),
            pltpu.VMEM((5, depth, depth), F32),
            pltpu.VMEM((8, depth), F32),
        ],
        compiler_params=pltpu.CompilerParams(vmem_limit_bytes=VMEM_BYTES),
        cost_estimate=pl.CostEstimate(
            flops=pairs * 64 * lines * lines * HEAD_DIM,
            bytes_accessed=14 << 20,
            transcendentals=0,
        ),
        name="attention_back",
    )(up, amino, core, *saved, wq, wk, wv, wg, wo, gain)


def combine_kernel(core_ref, keep_ref, got_ref, out_ref):
    total = keep_ref[:, MSA:, :].astype(F32) + got_ref[:, MSA:, :].astype(F32)
    out_ref[...] = total.astype(BF16)


def combine(core, keep, got):
    return pl.pallas_call(
        combine_kernel,
        out_shape=shape((keep.shape[0], PIECE, LANES), BF16),
        in_specs=[SMEM] + specs(2),
        out_specs=specs(1)[0],
        compiler_params=pltpu.CompilerParams(vmem_limit_bytes=16 << 20),
        name="combine",
    )(core, keep, got)


def pack_kernel(core_ref, keep_ref, got_ref, after_ref, out_ref):
    low = core_ref[0] == 0
    for half in range(2):
        rows = slice(16 * half, 16 * half + 16)
        keep, got = keep_ref[:, rows, :], got_ref[:, rows, :]
        at = 32 * half
        out_ref[:, at : at + 16, :] = jnp.where(low, keep, got)
        out_ref[:, at + 16 : at + 32, :] = jnp.where(low, got, keep)


def pack(core, keep, got, after):
    return pl.pallas_call(
        pack_kernel,
        out_shape=shape((keep.shape[0], 2 * MSA, LANES), BF16),
        in_specs=[SMEM] + specs(2) + [pl.BlockSpec(memory_space=pl.ANY)],
        out_specs=specs(1)[0],
        compiler_params=pltpu.CompilerParams(vmem_limit_bytes=16 << 20),
        name="pack",
    )(core, keep, got, after)


def merge_kernel(parts_ref, out_ref):
    out_ref[...] = jnp.sum(parts_ref[...].astype(F32), 0).astype(BF16)


def merge(parts):
    return pl.pallas_call(
        merge_kernel,
        out_shape=shape((PIECE, LANES), BF16),
        in_specs=specs(1),
        out_specs=specs(1)[0],
        compiler_params=pltpu.CompilerParams(vmem_limit_bytes=16 << 20),
        name="merge",
    )(parts)


def spread_kernel(piece_ref, got_ref, after_ref, out_ref):
    total = piece_ref[...].astype(F32) + got_ref[...].astype(F32)
    out_ref[...] = jnp.broadcast_to(total[None], out_ref.shape).astype(BF16)


def spread(piece, got, after, copies):
    return pl.pallas_call(
        spread_kernel,
        out_shape=shape((copies, PIECE, LANES), BF16),
        in_specs=specs(2) + [pl.BlockSpec(memory_space=pl.ANY)],
        out_specs=specs(1)[0],
        compiler_params=pltpu.CompilerParams(vmem_limit_bytes=16 << 20),
        name="spread",
    )(piece, got, after)


def unpack_kernel(factor, core_ref, own_ref, other_ref, *out_refs):
    low = core_ref[0] == 0
    for half in range(2):
        lanes = slice(half * LANES, (half + 1) * LANES)
        first = low if half == 0 else jnp.logical_not(low)
        own = own_ref[...].astype(F32)
        other = other_ref[...].astype(F32)
        g = jnp.where(first, own, other) * factor
        depth = out_refs[0].shape[0]
        for i in range(5):
            out_refs[i][:, lanes] = g[:, 8 * i : 8 * i + 8, :].reshape(depth, LANES)
        out_refs[5][:, lanes] = g[0, 40:44, :]


def unpack(core, own, other, depth, factor):
    vm = pl.BlockSpec(memory_space=pltpu.VMEM)
    sm = pl.BlockSpec(memory_space=pltpu.SMEM)
    return pl.pallas_call(
        functools.partial(unpack_kernel, factor),
        out_shape=(jax.ShapeDtypeStruct((depth, depth), F32),) * 5
        + (jax.ShapeDtypeStruct((4, depth), F32),),
        in_specs=[sm, vm, vm],
        out_specs=(vm,) * 6,
        compiler_params=pltpu.CompilerParams(vmem_limit_bytes=32 << 20),
        name="unpack",
    )(core, own, other)


def exchange(a, axis, groups=None):
    return lax.all_to_all(
        a, axis, split_axis=0, concat_axis=0, tiled=True, axis_index_groups=groups
    )


def shards(x, up, hom, amino, wq, wk, wv, wg, bg, wo, gain, off):
    _, near, residues, depth = up.shape
    n_dp, n_dap = lax.axis_size("dp"), lax.axis_size("dap")
    lines, members = x.shape[1], x.shape[2]
    chips = n_dap // 2
    partner = [(i, i ^ 1) for i in range(n_dap)]
    same_core = [[2 * i + c for i in range(chips)] for c in range(2)]
    core = (lax.axis_index("dap") % 2).astype(jnp.int32).reshape(1)

    rows = jnp.transpose(up[0].reshape(near, n_dap, members, depth), (1, 2, 0, 3))
    local_up = exchange(rows.reshape(n_dap, members * near, depth), "dap")
    swapped = jnp.transpose(x[0], (1, 0, 2))
    gain, off, bg = gain[None], off[None], bg[None]
    saved = front(swapped, hom, wq, wk, wv, wg, bg, gain, off)
    keep, send = back(local_up, amino, core, saved, wq, wk, wv, wg, wo, gain)

    got = lax.ppermute(send, "dap", partner)
    parts = exchange(combine(core, keep, got), "dap", same_core)
    msa = exchange(pack(core, keep, got, parts), "dap", same_core)
    piece = merge(parts)
    near_z = [(i, i ^ 1) for i in range(n_dp)]
    near_x = [(i, i ^ 2) for i in range(n_dp)]
    mirror_x = [(i, n_dp - 2 - (i & ~1) + (i & 1)) for i in range(n_dp)]
    for pairs in (near_z, near_x):
        other = lax.ppermute(piece, "dp", pairs)
        piece = (piece.astype(F32) + other.astype(F32)).astype(BF16)
    pieces = spread(piece, lax.ppermute(piece, "dp", mirror_x), msa, chips)
    own = exchange(pieces, "dap", same_core)
    other = lax.ppermute(own, "dap", partner)
    factor = float((n_dp * lines * residues) ** (-0.5))
    grads = unpack(core, own, other, depth, factor)

    msa = msa.reshape(chips, depth // LANES, 2, members, near, LANES)
    adjoint = jnp.transpose(msa, (4, 0, 2, 3, 1, 5)).reshape(1, near, residues, depth)
    return (adjoint,) + tuple(grads)


def solution(mesh):
    in_specs = (
        P("dp", None, "dap", None),
        P("dp", "dap", None, None),
        P("dp", None),
        P("dp", "dap"),
    ) + (P(),) * 8
    out_specs = (P("dp", "dap", None, None),) + (P(),) * 6
    return jax.shard_map(shards, mesh=mesh, in_specs=in_specs, out_specs=out_specs, check_vma=False)
```

```python
import functools

import jax
import jax.numpy as jnp
from jax import lax
from jax.experimental import pallas as pl
from jax.experimental.pallas import tpu as pltpu
from jax.sharding import PartitionSpec as P

HEADS = 8
HEAD_DIM = 32
LANES = 128
PIECE = 24
MSA = 16
GROUP = 8
VMEM_BYTES = 60 << 20
EPS = 1e-05
MASKED = 1000000000.0
F32, BF16 = jnp.float32, jnp.bfloat16


def mm(left, right):
    return lax.dot_general(left, right, (((1,), (0,)), ((), ())), preferred_element_type=F32)


def against(left, weight):
    return lax.dot_general(left, weight, (((1,), (1,)), ((), ())), preferred_element_type=F32)


def row_sum(a):
    return jnp.sum(a, 0, keepdims=True)


def front_kernel(
    x_ref,
    hom_ref,
    wq_ref,
    wk_ref,
    wv_ref,
    wg_ref,
    bg_ref,
    gain_ref,
    off_ref,
    xhat_ref,
    inv_ref,
    nt_ref,
    k_ref,
    v_ref,
    qt_ref,
    gate_ref,
    att_ref,
    probs_ref,
    q_s,
):
    _, lines, depth = x_ref.shape
    group = probs_ref.shape[1]
    step = pl.program_id(1)
    bias = (hom_ref[...].astype(F32) - 1.0) * MASKED
    lane_head = lax.broadcasted_iota(jnp.int32, (1, depth), 1) // HEAD_DIM

    @pl.when(step == 0)
    def _():
        x = x_ref[0].astype(F32)
        centred = x - jnp.mean(x, -1, keepdims=True)
        inv = lax.rsqrt(jnp.mean(centred * centred, -1, keepdims=True) + EPS)
        xhat = centred * inv
        xhat_ref[0] = xhat
        inv_ref[0] = jnp.broadcast_to(inv, (lines, LANES))
        normed = (xhat * gain_ref[...] + off_ref[...]).astype(BF16)
        nt_ref[0] = normed.T
        query = (mm(normed, wq_ref[...]) * HEAD_DIM**-0.5).astype(BF16)
        q_s[...] = query
        qt_ref[0] = query.T
        k_ref[0] = mm(normed, wk_ref[...]).astype(BF16)
        v_ref[0] = mm(normed, wv_ref[...]).astype(BF16)
        gate_ref[0] = jax.nn.sigmoid(mm(normed, wg_ref[...]) + bg_ref[...])
        att_ref[0] = jnp.zeros((lines, depth), F32)

    for j in range(group):
        own = (lane_head == step * group + j).astype(F32).astype(BF16)
        raised = jnp.exp(against(q_s[...] * own, k_ref[0]) + bias)
        probs = raised * (1.0 / jnp.sum(raised, -1, keepdims=True))
        probs_b = probs.astype(BF16)
        probs_ref[0, j] = probs_b
        att_ref[0] += mm(probs_b, v_ref[0] * own)


def back_kernel(
    up_ref,
    amino_ref,
    core_ref,
    xhat_ref,
    inv_ref,
    nt_ref,
    k_ref,
    v_ref,
    qt_ref,
    gate_ref,
    att_ref,
    probs_ref,
    wq_ref,
    wk_ref,
    wv_ref,
    wg_ref,
    wo_ref,
    gain_ref,
    keep_ref,
    send_ref,
    up_s,
    do_s,
    dot_s,
    prod_s,
    dg_s,
    dq_s,
    dkt_s,
    dvt_s,
    out_s,
    grad_s,
    vec_s,
):
    members, lines, depth = up_s.shape
    group = probs_ref.shape[1]
    r, step = pl.program_id(0), pl.program_id(1)
    last = pl.num_programs(1) - 1
    lane_head = lax.broadcasted_iota(jnp.int32, (1, depth), 1) // HEAD_DIM

    def update():
        return (up_s[r] * amino_ref[0, r].astype(F32)).astype(BF16)

    @pl.when(jnp.logical_and(r == 0, step == 0))
    def _():
        up = up_ref[...].astype(F32)
        for i in range(members):
            up_s[i] = up[:, 8 * i : 8 * i + 8, :].reshape(lines, depth)
        grad_s[...] = jnp.zeros_like(grad_s)
        vec_s[...] = jnp.zeros_like(vec_s)

    @pl.when(step == 0)
    def _():
        dg_s[...] = against(update(), wo_ref[...])
        d_att = (dg_s[...] * gate_ref[0]).astype(BF16)
        do_s[...] = d_att
        dot_s[...] = d_att.T
        prod_s[...] = d_att.astype(F32) * att_ref[0]
        dq_s[...] = jnp.zeros_like(dq_s)

    for j in range(group):
        h = step * group + j
        mask = (lane_head == h).astype(F32)
        own = mask.astype(BF16)
        rows = pl.ds(pl.multiple_of(h * HEAD_DIM, HEAD_DIM), HEAD_DIM)
        probs_b = probs_ref[0, j]
        delta = jnp.sum(prod_s[...] * mask, -1, keepdims=True)
        d_probs = against(do_s[...] * own, v_ref[0])
        d_scores = (probs_b.astype(F32) * (d_probs - delta)).astype(BF16)
        dq_s[...] += mm(d_scores, k_ref[0] * own)
        dkt_s[rows, :] = mm(qt_ref[0, rows, :], d_scores).astype(BF16)
        dvt_s[rows, :] = mm(dot_s[rows, :], probs_b).astype(BF16)

    @pl.when(step == last)
    def _():
        att, gate, d_gated, xhat = att_ref[0], gate_ref[0], dg_s[...], xhat_ref[0]
        d_update = update()
        gated = (gate * att).astype(BF16)
        d_logit = (d_gated * att * gate * (1.0 - gate)).astype(BF16)
        dq = (dq_s[...] * HEAD_DIM**-0.5).astype(BF16)
        dk = dkt_s[...].T
        dv = dvt_s[...].T
        d_normed = (
            against(dq, wq_ref[...])
            + against(dk, wk_ref[...])
            + against(dv, wv_ref[...])
            + against(d_logit, wg_ref[...])
        )
        d_hat = d_normed * gain_ref[...]
        d_branch = inv_ref[0][:, :1] * (
            d_hat
            - jnp.mean(d_hat, -1, keepdims=True)
            - xhat * jnp.mean(d_hat * xhat, -1, keepdims=True)
        )
        out_s[r] = (up_s[r] + d_branch).reshape(lines // 8, 8, depth)
        normed_t = nt_ref[0]
        mats = (
            mm(normed_t, dq),
            mm(normed_t, dk),
            mm(normed_t, dv),
            mm(normed_t, d_logit),
            mm(gated.T, d_update),
        )
        vecs = (
            row_sum(d_logit.astype(F32)),
            row_sum(d_update.astype(F32)),
            row_sum(d_normed * xhat),
            row_sum(d_normed),
        )
        for i, g in enumerate(mats):
            grad_s[i] += g
        for i, g in enumerate(vecs):
            vec_s[i : i + 1, :] += g

    @pl.when(jnp.logical_and(r == members - 1, step == last))
    def _():
        low = core_ref[0] == 0
        chips = depth // 8
        rows = jnp.concatenate([out_s[i] for i in range(members)], 1)
        rows = rows.reshape(chips, 2, MSA, depth)
        pieces = []
        for half in range(2):
            lanes = slice(half * LANES, (half + 1) * LANES)
            parts = [grad_s[i][:, lanes].reshape(chips, 8, LANES) for i in range(5)]
            parts.append(jnp.broadcast_to(vec_s[:, lanes][None], (chips, 8, LANES)))
            left, right = jnp.concatenate(parts[:3], 1), jnp.concatenate(parts[3:], 1)
            pieces.append(jnp.concatenate([left, right], 2))
        zero = jnp.concatenate([rows[:, 0], pieces[0]], 1)
        one = jnp.concatenate([rows[:, 1], pieces[1]], 1)
        keep_ref[...] = jnp.where(low, zero, one).astype(BF16)
        send_ref[...] = jnp.where(low, one, zero).astype(BF16)


def specs(n):
    return [pl.BlockSpec(memory_space=pltpu.VMEM)] * n


SMEM = pl.BlockSpec(memory_space=pltpu.SMEM)


def shape(dims, dtype):
    return jax.ShapeDtypeStruct(dims, dtype)


def whole(a):
    return pl.BlockSpec(a.shape, lambda r, h: (0,) * len(a.shape))


def by_member(a):
    return pl.BlockSpec((1,) + a.shape[1:], lambda r, h: (r,) + (0,) * (len(a.shape) - 1))


def by_group(a):
    return pl.BlockSpec((1, GROUP) + a.shape[2:], lambda r, h: (r, h, 0, 0))


def front(x, hom, wq, wk, wv, wg, bg, gain, off):
    members, lines, depth = x.shape
    tall, wide = (members, lines, depth), (members, depth, lines)
    pairs = members * HEADS
    outs = (
        shape(tall, F32),
        shape((members, lines, LANES), F32),
        shape(wide, BF16),
        shape(tall, BF16),
        shape(tall, BF16),
        shape(wide, BF16),
        shape(tall, F32),
        shape(tall, F32),
        shape((members, HEADS, lines, lines), BF16),
    )
    return pl.pallas_call(
        front_kernel,
        grid=(members, HEADS // GROUP),
        out_shape=outs,
        in_specs=[by_member(x)] + [whole(a) for a in (hom, wq, wk, wv, wg, bg, gain, off)],
        out_specs=[by_member(a) for a in outs[:-1]] + [by_group(outs[-1])],
        scratch_shapes=[pltpu.VMEM((lines, depth), BF16)],
        compiler_params=pltpu.CompilerParams(vmem_limit_bytes=VMEM_BYTES),
        cost_estimate=pl.CostEstimate(
            flops=pairs * 32 * lines * lines * HEAD_DIM,
            bytes_accessed=14 << 20,
            transcendentals=pairs * lines * lines,
        ),
        name="attention_front",
    )(x, hom, wq, wk, wv, wg, bg, gain, off)


def back(up, amino, core, saved, wq, wk, wv, wg, wo, gain):
    members, lines, depth = saved[0].shape
    tall, wide = (lines, depth), (depth, lines)
    pairs = members * HEADS
    parcel = shape((depth // 8, MSA + PIECE, depth), BF16)
    return pl.pallas_call(
        back_kernel,
        grid=(members, HEADS // GROUP),
        out_shape=(parcel, parcel),
        in_specs=[whole(up), SMEM, SMEM]
        + [by_member(a) for a in saved[:-1]]
        + [by_group(saved[-1])]
        + [whole(a) for a in (wq, wk, wv, wg, wo, gain)],
        out_specs=[whole(parcel), whole(parcel)],
        scratch_shapes=[
            pltpu.VMEM((members,) + tall, F32),
            pltpu.VMEM(tall, BF16),
            pltpu.VMEM(wide, BF16),
            pltpu.VMEM(tall, F32),
            pltpu.VMEM(tall, F32),
            pltpu.VMEM(tall, F32),
            pltpu.VMEM(wide, BF16),
            pltpu.VMEM(wide, BF16),
            pltpu.VMEM((members, lines // 8, 8, depth), F32),
            pltpu.VMEM((5, depth, depth), F32),
            pltpu.VMEM((8, depth), F32),
        ],
        compiler_params=pltpu.CompilerParams(vmem_limit_bytes=VMEM_BYTES),
        cost_estimate=pl.CostEstimate(
            flops=pairs * 64 * lines * lines * HEAD_DIM,
            bytes_accessed=14 << 20,
            transcendentals=0,
        ),
        name="attention_back",
    )(up, amino, core, *saved, wq, wk, wv, wg, wo, gain)


def combine_kernel(core_ref, keep_ref, got_ref, out_ref):
    low = core_ref[0] == 0
    keep, got = keep_ref[...].astype(F32), got_ref[...].astype(F32)
    first = jnp.where(low, keep[:, :MSA], got[:, :MSA])
    second = jnp.where(low, got[:, :MSA], keep[:, :MSA])
    total = keep[:, MSA:] + got[:, MSA:]
    out_ref[...] = jnp.concatenate([first, second, total], 1).astype(BF16)


def combine(core, keep, got):
    chips, _, depth = keep.shape
    return pl.pallas_call(
        combine_kernel,
        out_shape=shape((chips, 2 * MSA + PIECE, depth), BF16),
        in_specs=[SMEM] + specs(2),
        out_specs=specs(1)[0],
        compiler_params=pltpu.CompilerParams(vmem_limit_bytes=24 << 20),
        name="combine",
    )(core, keep, got)


def merge_kernel(parts_ref, out_ref):
    start = parts_ref.shape[1] - PIECE
    total = jnp.sum(parts_ref[...].astype(F32)[:, start:], 0, keepdims=True)
    out_ref[...] = jnp.broadcast_to(total, out_ref.shape).astype(BF16)


def merge(parts, copies):
    return pl.pallas_call(
        merge_kernel,
        out_shape=shape((copies, PIECE, parts.shape[2]), BF16),
        in_specs=specs(1),
        out_specs=specs(1)[0],
        compiler_params=pltpu.CompilerParams(vmem_limit_bytes=24 << 20),
        name="merge",
    )(parts)


def gather_kernel(up_ref, out_ref, rows_s):
    near, residues, depth = up_ref.shape
    for half in range(depth // LANES):
        lanes = slice(half * LANES, (half + 1) * LANES)
        rows_s[...] = up_ref[:, :, lanes].astype(F32).reshape(near * residues, LANES)
        for n in range(0, residues, 2):
            pair = [rows_s[pl.ds(n + r, near, stride=residues), :] for r in range(2)]
            out_ref[n // 2, :, lanes] = jnp.concatenate(pair, 0).astype(BF16)


def gather_rows(up):
    near, residues, depth = up.shape
    return pl.pallas_call(
        gather_kernel,
        out_shape=shape((residues // 2, 2 * near, depth), BF16),
        in_specs=specs(1),
        out_specs=specs(1)[0],
        scratch_shapes=[pltpu.VMEM((near * residues, LANES), F32)],
        compiler_params=pltpu.CompilerParams(vmem_limit_bytes=16 << 20),
        name="gather_rows",
    )(up)


def unpack_kernel(factor, core_ref, own_ref, other_ref, *out_refs):
    low = core_ref[0] == 0
    own, other = own_ref[...].astype(F32), other_ref[...].astype(F32)
    depth = out_refs[0].shape[0]
    for half in range(2):
        lanes = slice(half * LANES, (half + 1) * LANES)
        first = low if half == 0 else jnp.logical_not(low)
        g = jnp.where(first, own, other) * factor
        for i in range(6):
            side, at = i // 3, 8 * (i % 3)
            block = g[:, at : at + 8, side * LANES : (side + 1) * LANES]
            if i < 5:
                out_refs[i][:, lanes] = block.reshape(depth, LANES)
            else:
                out_refs[i][:, lanes] = block[0, :4]


def unpack(core, own, other, depth, factor):
    vm = pl.BlockSpec(memory_space=pltpu.VMEM)
    sm = pl.BlockSpec(memory_space=pltpu.SMEM)
    return pl.pallas_call(
        functools.partial(unpack_kernel, factor),
        out_shape=(jax.ShapeDtypeStruct((depth, depth), F32),) * 5
        + (jax.ShapeDtypeStruct((4, depth), F32),),
        in_specs=[sm, vm, vm],
        out_specs=(vm,) * 6,
        compiler_params=pltpu.CompilerParams(vmem_limit_bytes=32 << 20),
        name="unpack",
    )(core, own, other)


def exchange(a, axis, groups=None):
    return lax.all_to_all(
        a, axis, split_axis=0, concat_axis=0, tiled=True, axis_index_groups=groups
    )


def shards(x, up, hom, amino, wq, wk, wv, wg, bg, wo, gain, off):
    _, near, residues, depth = up.shape
    n_dp, n_dap = lax.axis_size("dp"), lax.axis_size("dap")
    lines, members = x.shape[1], x.shape[2]
    chips = n_dap // 2
    partner = [(i, i ^ 1) for i in range(n_dap)]
    same_core = [[2 * i + c for i in range(chips)] for c in range(2)]
    core = (lax.axis_index("dap") % 2).astype(jnp.int32).reshape(1)

    local_up = exchange(gather_rows(up[0]), "dap")
    swapped = jnp.transpose(x[0], (1, 0, 2))
    gain, off, bg = gain[None], off[None], bg[None]
    saved = front(swapped, hom, wq, wk, wv, wg, bg, gain, off)
    keep, send = back(local_up, amino, core, saved, wq, wk, wv, wg, wo, gain)

    got = lax.ppermute(send, "dap", partner)
    parts = exchange(combine(core, keep, got), "dap", same_core)
    pieces = exchange(merge(parts, n_dp), "dp")
    own = exchange(merge(pieces, chips), "dap", same_core)
    other = lax.ppermute(own, "dap", partner)
    factor = float((n_dp * lines * residues) ** (-0.5))
    grads = unpack(core, own, other, depth, factor)

    msa = parts[:, : 2 * MSA].reshape(chips, 2, members, near, depth)
    adjoint = jnp.transpose(msa, (3, 0, 1, 2, 4)).reshape(1, near, residues, depth)
    return (adjoint,) + tuple(grads)


def solution(mesh):
    in_specs = (
        P("dp", None, "dap", None),
        P("dp", "dap", None, None),
        P("dp", None),
        P("dp", "dap"),
    ) + (P(),) * 8
    out_specs = (P("dp", "dap", None, None),) + (P(),) * 6
    return jax.shard_map(shards, mesh=mesh, in_specs=in_specs, out_specs=out_specs, check_vma=False)
```

```python
import functools

import jax
import jax.numpy as jnp
from jax import lax
from jax.experimental import pallas as pl
from jax.experimental.pallas import tpu as pltpu
from jax.sharding import PartitionSpec as P

HEADS = 8
HEAD_DIM = 32
LANES = 128
PIECE = 24
MSA = 16
GROUP = 8
VMEM_BYTES = 60 << 20
FRONT_BYTES = 51 << 20
BACK_BYTES = 50 << 20
EPS = 1e-05
MASKED = 1000000000.0
F32, BF16 = jnp.float32, jnp.bfloat16


def mm(left, right):
    return lax.dot_general(left, right, (((1,), (0,)), ((), ())), preferred_element_type=F32)


def against(left, weight):
    return lax.dot_general(left, weight, (((1,), (1,)), ((), ())), preferred_element_type=F32)


def row_sum(a):
    return jnp.sum(a, 0, keepdims=True)


def front_kernel(
    x_ref,
    *refs,
):
    ins, outs, scratch = refs[:8], refs[8:17], refs[17:]
    xhat_ref, inv_ref, nt_ref, k_ref, v_ref, qt_ref, gate_ref, att_ref, probs_ref = outs
    bufs, (q_s, sems) = scratch[:8], scratch[8:]
    hom_ref, wq_ref, wk_ref, wv_ref, wg_ref, bg_ref, gain_ref, off_ref = bufs
    _, lines, depth = x_ref.shape
    group = probs_ref.shape[1]
    r = pl.program_id(0)
    loads = [pltpu.make_async_copy(ins[i], bufs[i], sems.at[i]) for i in range(8)]
    step = pl.program_id(1)
    lane_head = lax.broadcasted_iota(jnp.int32, (1, depth), 1) // HEAD_DIM

    @pl.when(step == 0)
    def _():
        @pl.when(r == 0)
        def _():
            for load in loads:
                load.start()

        x = x_ref[0].astype(F32)
        centred = x - jnp.mean(x, -1, keepdims=True)
        inv = lax.rsqrt(jnp.mean(centred * centred, -1, keepdims=True) + EPS)
        xhat = centred * inv

        @pl.when(r == 0)
        def _():
            for load in loads:
                load.wait()

        xhat_ref[0] = xhat
        inv_ref[0] = jnp.broadcast_to(inv, (lines, LANES)).T[:8]
        normed = (xhat * gain_ref[...] + off_ref[...]).astype(BF16)
        nt_ref[0] = normed.T
        query = (mm(normed, wq_ref[...]) * HEAD_DIM**-0.5).astype(BF16)
        q_s[...] = query
        qt_ref[0] = query.T
        k_ref[0] = mm(normed, wk_ref[...]).astype(BF16)
        v_ref[0] = mm(normed, wv_ref[...]).astype(BF16)
        gate_ref[0] = jax.nn.sigmoid(mm(normed, wg_ref[...]) + bg_ref[...])
        att_ref[0] = jnp.zeros((lines, depth), F32)

    bias = (hom_ref[...].astype(F32) - 1.0) * MASKED
    for j in range(group):
        own = (lane_head == step * group + j).astype(F32).astype(BF16)
        raised = jnp.exp(against(q_s[...] * own, k_ref[0]) + bias)
        probs = raised * (1.0 / jnp.sum(raised, -1, keepdims=True))
        probs_b = probs.astype(BF16)
        probs_ref[0, j] = probs_b
        att_ref[0] += mm(probs_b, v_ref[0] * own)


def back_kernel(
    up_ref,
    amino_ref,
    core_ref,
    xhat_ref,
    inv_ref,
    nt_ref,
    k_ref,
    v_ref,
    qt_ref,
    gate_ref,
    att_ref,
    probs_ref,
    wq_ref,
    wk_ref,
    wv_ref,
    wg_ref,
    wo_ref,
    gain_ref,
    keep_ref,
    send_ref,
    up_s,
    do_s,
    dot_s,
    prod_s,
    dg_s,
    dq_s,
    dkt_s,
    dvt_s,
    out_s,
    grad_s,
    vec_s,
):
    members, lines, depth = up_s.shape
    group = probs_ref.shape[1]
    r, step = pl.program_id(0), pl.program_id(1)
    last = pl.num_programs(1) - 1
    lane_head = lax.broadcasted_iota(jnp.int32, (1, depth), 1) // HEAD_DIM

    def update():
        return (up_s[r] * amino_ref[0, r].astype(F32)).astype(BF16)

    @pl.when(jnp.logical_and(r == 0, step == 0))
    def _():
        up = up_ref[...].astype(F32)
        for i in range(members):
            up_s[i] = up[:, 8 * i : 8 * i + 8, :].reshape(lines, depth)
        grad_s[...] = jnp.zeros_like(grad_s)
        vec_s[...] = jnp.zeros_like(vec_s)

    @pl.when(step == 0)
    def _():
        dg_s[...] = against(update(), wo_ref[...])
        d_att = (dg_s[...] * gate_ref[0]).astype(BF16)
        do_s[...] = d_att
        dot_s[...] = d_att.T
        prod_s[...] = d_att.astype(F32) * att_ref[0]
        dq_s[...] = jnp.zeros_like(dq_s)

    for j in range(group):
        h = step * group + j
        mask = (lane_head == h).astype(F32)
        own = mask.astype(BF16)
        rows = pl.ds(pl.multiple_of(h * HEAD_DIM, HEAD_DIM), HEAD_DIM)
        probs_b = probs_ref[0, j]
        delta = jnp.sum(prod_s[...] * mask, -1, keepdims=True)
        d_probs = against(do_s[...] * own, v_ref[0])
        d_scores = (probs_b.astype(F32) * (d_probs - delta)).astype(BF16)
        dq_s[...] += mm(d_scores, k_ref[0] * own)
        dkt_s[rows, :] = mm(qt_ref[0, rows, :], d_scores).astype(BF16)
        dvt_s[rows, :] = mm(dot_s[rows, :], probs_b).astype(BF16)

    @pl.when(step == last)
    def _():
        att, gate, d_gated, xhat = att_ref[0], gate_ref[0], dg_s[...], xhat_ref[0]
        d_update = update()
        gated = (gate * att).astype(BF16)
        d_logit = (d_gated * att * gate * (1.0 - gate)).astype(BF16)
        dq = (dq_s[...] * HEAD_DIM**-0.5).astype(BF16)
        dk = dkt_s[...].T
        dv = dvt_s[...].T
        d_normed = (
            against(dq, wq_ref[...])
            + against(dk, wk_ref[...])
            + against(dv, wv_ref[...])
            + against(d_logit, wg_ref[...])
        )
        d_hat = d_normed * gain_ref[...]
        d_branch = inv_ref[0].T[:, :1] * (
            d_hat
            - jnp.mean(d_hat, -1, keepdims=True)
            - xhat * jnp.mean(d_hat * xhat, -1, keepdims=True)
        )
        out_s[r] = (up_s[r] + d_branch).reshape(lines // 8, 8, depth)
        normed_t = nt_ref[0]
        mats = (
            mm(normed_t, dq),
            mm(normed_t, dk),
            mm(normed_t, dv),
            mm(normed_t, d_logit),
            mm(gated.T, d_update),
        )
        vecs = (
            row_sum(d_logit.astype(F32)),
            row_sum(d_update.astype(F32)),
            row_sum(d_normed * xhat),
            row_sum(d_normed),
        )
        for i, g in enumerate(mats):
            grad_s[i] += g
        for i, g in enumerate(vecs):
            vec_s[i : i + 1, :] += g

    @pl.when(jnp.logical_and(r == members - 1, step == last))
    def _():
        low = core_ref[0] == 0
        chips = depth // 8
        rows = jnp.concatenate([out_s[i] for i in range(members)], 1)
        rows = rows.reshape(chips, 2, MSA, depth)
        pieces = []
        for half in range(2):
            lanes = slice(half * LANES, (half + 1) * LANES)
            parts = [grad_s[i][:, lanes].reshape(chips, 8, LANES) for i in range(5)]
            parts.append(jnp.broadcast_to(vec_s[:, lanes][None], (chips, 8, LANES)))
            left, right = jnp.concatenate(parts[:3], 1), jnp.concatenate(parts[3:], 1)
            pieces.append(jnp.concatenate([left, right], 2))
        zero = jnp.concatenate([rows[:, 0], pieces[0]], 1)
        one = jnp.concatenate([rows[:, 1], pieces[1]], 1)
        keep_ref[...] = jnp.where(low, zero, one).astype(BF16)
        send_ref[...] = jnp.where(low, one, zero).astype(BF16)


def specs(n):
    return [pl.BlockSpec(memory_space=pltpu.VMEM)] * n


SMEM = pl.BlockSpec(memory_space=pltpu.SMEM)
HBM = pl.BlockSpec(memory_space=pltpu.HBM)


def shape(dims, dtype):
    return jax.ShapeDtypeStruct(dims, dtype)


def in_hbm(a):
    return pltpu.with_memory_space_constraint(a, pltpu.HBM)


def whole(a):
    return pl.BlockSpec(a.shape, lambda r, h: (0,) * len(a.shape))


def by_member(a):
    return pl.BlockSpec((1,) + a.shape[1:], lambda r, h: (r,) + (0,) * (len(a.shape) - 1))


def by_group(a):
    return pl.BlockSpec((1, GROUP) + a.shape[2:], lambda r, h: (r, h, 0, 0))


def front(x, hom, wq, wk, wv, wg, bg, gain, off):
    fixed = (hom, wq, wk, wv, wg, bg, gain, off)
    fixed = tuple(in_hbm(a) for a in fixed)
    members, lines, depth = x.shape
    tall, wide = (members, lines, depth), (members, depth, lines)
    pairs = members * HEADS
    outs = (
        shape(tall, F32),
        shape((members, 8, lines), F32),
        shape(wide, BF16),
        shape(tall, BF16),
        shape(tall, BF16),
        shape(wide, BF16),
        shape(tall, F32),
        shape(tall, F32),
        shape((members, HEADS, lines, lines), BF16),
    )
    return pl.pallas_call(
        front_kernel,
        grid=(members, HEADS // GROUP),
        out_shape=outs,
        in_specs=[by_member(x)] + [HBM] * len(fixed),
        out_specs=[by_member(a) for a in outs[:-1]] + [by_group(outs[-1])],
        scratch_shapes=[pltpu.VMEM(a.shape, a.dtype) for a in fixed]
        + [pltpu.VMEM((lines, depth), BF16), pltpu.SemaphoreType.DMA((len(fixed),))],
        compiler_params=pltpu.CompilerParams(vmem_limit_bytes=FRONT_BYTES),
        cost_estimate=pl.CostEstimate(
            flops=pairs * 32 * lines * lines * HEAD_DIM,
            bytes_accessed=14 << 20,
            transcendentals=pairs * lines * lines,
        ),
        name="attention_front",
    )(x, *fixed)


def back(up, amino, core, saved, wq, wk, wv, wg, wo, gain):
    xhat, inv, nt, k, v, qt, gate, att, probs = saved
    saved = (in_hbm(xhat), inv, nt, k, v, *(in_hbm(a) for a in (qt, gate, att, probs)))
    members, lines, depth = xhat.shape
    tall, wide = (lines, depth), (depth, lines)
    pairs = members * HEADS
    parcel = shape((depth // 8, MSA + PIECE, depth), BF16)
    return pl.pallas_call(
        back_kernel,
        grid=(members, HEADS // GROUP),
        out_shape=(parcel, parcel),
        in_specs=[whole(up), SMEM, SMEM]
        + [by_member(a) for a in saved[:-1]]
        + [by_group(saved[-1])]
        + [whole(a) for a in (wq, wk, wv, wg, wo, gain)],
        out_specs=[whole(parcel), whole(parcel)],
        scratch_shapes=[
            pltpu.VMEM((members,) + tall, F32),
            pltpu.VMEM(tall, BF16),
            pltpu.VMEM(wide, BF16),
            pltpu.VMEM(tall, F32),
            pltpu.VMEM(tall, F32),
            pltpu.VMEM(tall, F32),
            pltpu.VMEM(wide, BF16),
            pltpu.VMEM(wide, BF16),
            pltpu.VMEM((members, lines // 8, 8, depth), F32),
            pltpu.VMEM((5, depth, depth), F32),
            pltpu.VMEM((8, depth), F32),
        ],
        compiler_params=pltpu.CompilerParams(vmem_limit_bytes=BACK_BYTES),
        cost_estimate=pl.CostEstimate(
            flops=pairs * 64 * lines * lines * HEAD_DIM,
            bytes_accessed=14 << 20,
            transcendentals=0,
        ),
        name="attention_back",
    )(up, amino, core, *saved, wq, wk, wv, wg, wo, gain)


def combine_kernel(core_ref, keep_ref, got_ref, out_ref):
    low = core_ref[0] == 0
    keep, got = keep_ref[...].astype(F32), got_ref[...].astype(F32)
    first = jnp.where(low, keep[:, :MSA], got[:, :MSA])
    second = jnp.where(low, got[:, :MSA], keep[:, :MSA])
    total = keep[:, MSA:] + got[:, MSA:]
    out_ref[...] = jnp.concatenate([first, second, total], 1).astype(BF16)


def combine(core, keep, got):
    chips, _, depth = keep.shape
    return pl.pallas_call(
        combine_kernel,
        out_shape=shape((chips, 2 * MSA + PIECE, depth), BF16),
        in_specs=[SMEM] + specs(2),
        out_specs=specs(1)[0],
        compiler_params=pltpu.CompilerParams(vmem_limit_bytes=24 << 20),
        name="combine",
    )(core, keep, got)


def merge_kernel(parts_ref, out_ref):
    start = parts_ref.shape[1] - PIECE
    total = jnp.sum(parts_ref[...].astype(F32)[:, start:], 0, keepdims=True)
    out_ref[...] = jnp.broadcast_to(total, out_ref.shape).astype(BF16)


def merge(parts, copies):
    return pl.pallas_call(
        merge_kernel,
        out_shape=shape((copies, PIECE, parts.shape[2]), BF16),
        in_specs=specs(1),
        out_specs=specs(1)[0],
        compiler_params=pltpu.CompilerParams(vmem_limit_bytes=24 << 20),
        name="merge",
    )(parts)


def gather_kernel(up_ref, out_ref, rows_s):
    near, residues, depth = up_ref.shape
    for half in range(depth // LANES):
        lanes = slice(half * LANES, (half + 1) * LANES)
        rows_s[...] = up_ref[:, :, lanes].astype(F32).reshape(near * residues, LANES)
        for n in range(0, residues, 2):
            pair = [rows_s[pl.ds(n + r, near, stride=residues), :] for r in range(2)]
            out_ref[n // 2, :, lanes] = jnp.concatenate(pair, 0).astype(BF16)


def gather_rows(up):
    near, residues, depth = up.shape
    return pl.pallas_call(
        gather_kernel,
        out_shape=shape((residues // 2, 2 * near, depth), BF16),
        in_specs=specs(1),
        out_specs=specs(1)[0],
        scratch_shapes=[pltpu.VMEM((near * residues, LANES), F32)],
        compiler_params=pltpu.CompilerParams(vmem_limit_bytes=VMEM_BYTES),
        name="gather_rows",
    )(up)


def unpack_kernel(factor, core_ref, own_ref, other_ref, *out_refs):
    low = core_ref[0] == 0
    own, other = own_ref[...].astype(F32), other_ref[...].astype(F32)
    depth = out_refs[0].shape[0]
    for half in range(2):
        lanes = slice(half * LANES, (half + 1) * LANES)
        first = low if half == 0 else jnp.logical_not(low)
        g = jnp.where(first, own, other) * factor
        for i in range(6):
            side, at = i // 3, 8 * (i % 3)
            block = g[:, at : at + 8, side * LANES : (side + 1) * LANES]
            if i < 5:
                out_refs[i][:, lanes] = block.reshape(depth, LANES)
            else:
                out_refs[i][:, lanes] = block[0, :4]


def unpack(core, own, other, depth, factor):
    vm = pl.BlockSpec(memory_space=pltpu.VMEM)
    sm = pl.BlockSpec(memory_space=pltpu.SMEM)
    return pl.pallas_call(
        functools.partial(unpack_kernel, factor),
        out_shape=(jax.ShapeDtypeStruct((depth, depth), F32),) * 5
        + (jax.ShapeDtypeStruct((4, depth), F32),),
        in_specs=[sm, vm, vm],
        out_specs=(vm,) * 6,
        compiler_params=pltpu.CompilerParams(vmem_limit_bytes=32 << 20),
        name="unpack",
    )(core, own, other)


def exchange(a, axis, groups=None):
    return lax.all_to_all(
        a, axis, split_axis=0, concat_axis=0, tiled=True, axis_index_groups=groups
    )


def shards(x, up, hom, amino, wq, wk, wv, wg, bg, wo, gain, off):
    _, near, residues, depth = up.shape
    n_dp, n_dap = lax.axis_size("dp"), lax.axis_size("dap")
    lines, members = x.shape[1], x.shape[2]
    chips = n_dap // 2
    partner = [(i, i ^ 1) for i in range(n_dap)]
    same_core = [[2 * i + c for i in range(chips)] for c in range(2)]
    core = (lax.axis_index("dap") % 2).astype(jnp.int32).reshape(1)

    local_up = exchange(gather_rows(up[0]), "dap")
    swapped = jnp.transpose(x[0], (1, 0, 2))
    gain, off, bg = gain[None], off[None], bg[None]
    saved = front(swapped, hom, wq, wk, wv, wg, bg, gain, off)
    keep, send = back(local_up, amino, core, saved, wq, wk, wv, wg, wo, gain)

    got = lax.ppermute(send, "dap", partner)
    parts = exchange(combine(core, keep, got), "dap", same_core)
    pieces = exchange(merge(parts, n_dp), "dp")
    own = exchange(merge(pieces, chips), "dap", same_core)
    other = lax.ppermute(own, "dap", partner)
    factor = float((n_dp * lines * residues) ** (-0.5))
    grads = unpack(core, own, other, depth, factor)

    msa = parts[:, : 2 * MSA].reshape(chips, 2, members, near, depth)
    adjoint = jnp.transpose(msa, (3, 0, 1, 2, 4)).reshape(1, near, residues, depth)
    return (adjoint,) + tuple(grads)


def solution(mesh):
    in_specs = (
        P("dp", None, "dap", None),
        P("dp", "dap", None, None),
        P("dp", None),
        P("dp", "dap"),
    ) + (P(),) * 8
    out_specs = (P("dp", "dap", None, None),) + (P(),) * 6
    return jax.shard_map(shards, mesh=mesh, in_specs=in_specs, out_specs=out_specs, check_vma=False)
```

```python
import functools

import jax
import jax.numpy as jnp
from jax import lax
from jax.experimental import pallas as pl
from jax.experimental.pallas import tpu as pltpu
from jax.sharding import PartitionSpec as P

HEADS = 8
HEAD_DIM = 32
LANES = 128
PIECE = 24
MSA = 16
GROUP = 8
VMEM_BYTES = 60 << 20
FRONT_BYTES = 51 << 20
BACK_BYTES = 50 << 20
EPS = 1e-05
MASKED = 1000000000.0
F32, BF16 = jnp.float32, jnp.bfloat16


def mm(left, right):
    return lax.dot_general(left, right, (((1,), (0,)), ((), ())), preferred_element_type=F32)


def against(left, weight):
    return lax.dot_general(left, weight, (((1,), (1,)), ((), ())), preferred_element_type=F32)


def row_sum(a):
    return jnp.sum(a, 0, keepdims=True)


def front_kernel(
    x_ref,
    *refs,
):
    ins, outs, scratch = refs[:8], refs[8:17], refs[17:]
    xhat_ref, inv_ref, nt_ref, k_ref, v_ref, qt_ref, gate_ref, att_ref, probs_ref = outs
    bufs, (q_s, sems) = scratch[:8], scratch[8:]
    hom_ref, wq_ref, wk_ref, wv_ref, wg_ref, bg_ref, gain_ref, off_ref = bufs
    _, lines, depth = x_ref.shape
    group = probs_ref.shape[1]
    r = pl.program_id(0)
    loads = [pltpu.make_async_copy(ins[i], bufs[i], sems.at[i]) for i in range(8)]
    step = pl.program_id(1)
    lane_head = lax.broadcasted_iota(jnp.int32, (1, depth), 1) // HEAD_DIM

    @pl.when(step == 0)
    def _():
        @pl.when(r == 0)
        def _():
            for load in loads:
                load.start()

        x = x_ref[0].astype(F32)
        centred = x - jnp.mean(x, -1, keepdims=True)
        inv = lax.rsqrt(jnp.mean(centred * centred, -1, keepdims=True) + EPS)
        xhat = centred * inv

        @pl.when(r == 0)
        def _():
            for load in loads:
                load.wait()

        xhat_ref[0] = xhat
        inv_ref[0] = jnp.broadcast_to(inv, (lines, LANES)).T[:8]
        normed = (xhat * gain_ref[...] + off_ref[...]).astype(BF16)
        nt_ref[0] = normed.T
        query = (mm(normed, wq_ref[...]) * HEAD_DIM**-0.5).astype(BF16)
        q_s[...] = query
        qt_ref[0] = query.T
        k_ref[0] = mm(normed, wk_ref[...]).astype(BF16)
        v_ref[0] = mm(normed, wv_ref[...]).astype(BF16)
        gate_ref[0] = jax.nn.sigmoid(mm(normed, wg_ref[...]) + bg_ref[...])
        att_ref[0] = jnp.zeros((lines, depth), F32)

    bias = (hom_ref[...].astype(F32) - 1.0) * MASKED
    for j in range(group):
        own = (lane_head == step * group + j).astype(F32).astype(BF16)
        raised = jnp.exp(against(q_s[...] * own, k_ref[0]) + bias)
        probs = raised * (1.0 / jnp.sum(raised, -1, keepdims=True))
        probs_b = probs.astype(BF16)
        probs_ref[0, j] = probs_b
        att_ref[0] += mm(probs_b, v_ref[0] * own)


def back_kernel(
    up_ref,
    amino_ref,
    core_ref,
    xhat_ref,
    inv_ref,
    nt_ref,
    k_ref,
    v_ref,
    qt_ref,
    gate_ref,
    att_ref,
    probs_ref,
    wq_ref,
    wk_ref,
    wv_ref,
    wg_ref,
    wo_ref,
    gain_ref,
    keep_ref,
    send_ref,
    up_s,
    do_s,
    dot_s,
    prod_s,
    dg_s,
    dq_s,
    dkt_s,
    dvt_s,
    out_s,
    grad_s,
    vec_s,
):
    members, lines, depth = up_s.shape
    group = probs_ref.shape[1]
    r, step = pl.program_id(0), pl.program_id(1)
    last = pl.num_programs(1) - 1
    lane_head = lax.broadcasted_iota(jnp.int32, (1, depth), 1) // HEAD_DIM

    def update():
        return (up_s[r] * amino_ref[0, r].astype(F32)).astype(BF16)

    @pl.when(jnp.logical_and(r == 0, step == 0))
    def _():
        up = up_ref[...].astype(F32)
        for i in range(members):
            up_s[i] = up[:, 8 * i : 8 * i + 8, :].reshape(lines, depth)
        grad_s[...] = jnp.zeros_like(grad_s)
        vec_s[...] = jnp.zeros_like(vec_s)

    @pl.when(step == 0)
    def _():
        dg_s[...] = against(update(), wo_ref[...])
        d_att = (dg_s[...] * gate_ref[0]).astype(BF16)
        do_s[...] = d_att
        dot_s[...] = d_att.T
        prod_s[...] = d_att.astype(F32) * att_ref[0]
        dq_s[...] = jnp.zeros_like(dq_s)

    for j in range(group):
        h = step * group + j
        mask = (lane_head == h).astype(F32)
        own = mask.astype(BF16)
        rows = pl.ds(pl.multiple_of(h * HEAD_DIM, HEAD_DIM), HEAD_DIM)
        probs_b = probs_ref[0, j]
        delta = jnp.sum(prod_s[...] * mask, -1, keepdims=True)
        d_probs = against(do_s[...] * own, v_ref[0])
        d_scores = (probs_b.astype(F32) * (d_probs - delta)).astype(BF16)
        dq_s[...] += mm(d_scores, k_ref[0] * own)
        dkt_s[rows, :] = mm(qt_ref[0, rows, :], d_scores).astype(BF16)
        dvt_s[rows, :] = mm(dot_s[rows, :], probs_b).astype(BF16)

    @pl.when(step == last)
    def _():
        att, gate, d_gated, xhat = att_ref[0], gate_ref[0], dg_s[...], xhat_ref[0]
        d_update = update()
        gated = (gate * att).astype(BF16)
        d_logit = (d_gated * att * gate * (1.0 - gate)).astype(BF16)
        dq = (dq_s[...] * HEAD_DIM**-0.5).astype(BF16)
        dk = dkt_s[...].T
        dv = dvt_s[...].T
        d_normed = (
            against(dq, wq_ref[...])
            + against(dk, wk_ref[...])
            + against(dv, wv_ref[...])
            + against(d_logit, wg_ref[...])
        )
        d_hat = d_normed * gain_ref[...]
        d_branch = inv_ref[0].T[:, :1] * (
            d_hat
            - jnp.mean(d_hat, -1, keepdims=True)
            - xhat * jnp.mean(d_hat * xhat, -1, keepdims=True)
        )
        out_s[r] = (up_s[r] + d_branch).reshape(lines // 8, 8, depth)
        normed_t = nt_ref[0]
        mats = (
            mm(normed_t, dq),
            mm(normed_t, dk),
            mm(normed_t, dv),
            mm(normed_t, d_logit),
            mm(gated.T, d_update),
        )
        vecs = (
            row_sum(d_logit.astype(F32)),
            row_sum(d_update.astype(F32)),
            row_sum(d_normed * xhat),
            row_sum(d_normed),
        )
        for i, g in enumerate(mats):
            grad_s[i] += g
        for i, g in enumerate(vecs):
            vec_s[i : i + 1, :] += g

    @pl.when(jnp.logical_and(r == members - 1, step == last))
    def _():
        low = core_ref[0] == 0
        chips = depth // 8
        rows = jnp.concatenate([out_s[i] for i in range(members)], 1)
        rows = rows.reshape(chips, 2, MSA, depth)
        vecs = jnp.concatenate([vec_s[:4, :LANES], vec_s[:4, LANES:]], 0)
        pieces = []
        for half in range(2):
            lanes = slice(half * LANES, (half + 1) * LANES)
            parts = [grad_s[i][:, lanes].reshape(chips, 8, LANES) for i in range(5)]
            parts.append(jnp.broadcast_to(vecs[None], (chips, 8, LANES)))
            left, right = jnp.concatenate(parts[:3], 1), jnp.concatenate(parts[3:], 1)
            pieces.append(jnp.concatenate([left, right], 2))
        zero = jnp.concatenate([rows[:, 0], pieces[0]], 1)
        one = jnp.concatenate([rows[:, 1], pieces[1]], 1)
        keep_ref[...] = jnp.where(low, zero, one).astype(BF16)
        send_ref[...] = jnp.where(low, one, zero).astype(BF16)


def specs(n):
    return [pl.BlockSpec(memory_space=pltpu.VMEM)] * n


SMEM = pl.BlockSpec(memory_space=pltpu.SMEM)
HBM = pl.BlockSpec(memory_space=pltpu.HBM)


def shape(dims, dtype):
    return jax.ShapeDtypeStruct(dims, dtype)


def in_hbm(a):
    return pltpu.with_memory_space_constraint(a, pltpu.HBM)


def whole(a):
    return pl.BlockSpec(a.shape, lambda r, h: (0,) * len(a.shape))


def by_member(a):
    return pl.BlockSpec((1,) + a.shape[1:], lambda r, h: (r,) + (0,) * (len(a.shape) - 1))


def by_group(a):
    return pl.BlockSpec((1, GROUP) + a.shape[2:], lambda r, h: (r, h, 0, 0))


def front(x, hom, wq, wk, wv, wg, bg, gain, off):
    fixed = (hom, wq, wk, wv, wg, bg, gain, off)
    fixed = tuple(in_hbm(a) for a in fixed)
    members, lines, depth = x.shape
    tall, wide = (members, lines, depth), (members, depth, lines)
    pairs = members * HEADS
    outs = (
        shape(tall, F32),
        shape((members, 8, lines), F32),
        shape(wide, BF16),
        shape(tall, BF16),
        shape(tall, BF16),
        shape(wide, BF16),
        shape(tall, F32),
        shape(tall, F32),
        shape((members, HEADS, lines, lines), BF16),
    )
    return pl.pallas_call(
        front_kernel,
        grid=(members, HEADS // GROUP),
        out_shape=outs,
        in_specs=[by_member(x)] + [HBM] * len(fixed),
        out_specs=[by_member(a) for a in outs[:-1]] + [by_group(outs[-1])],
        scratch_shapes=[pltpu.VMEM(a.shape, a.dtype) for a in fixed]
        + [pltpu.VMEM((lines, depth), BF16), pltpu.SemaphoreType.DMA((len(fixed),))],
        compiler_params=pltpu.CompilerParams(vmem_limit_bytes=FRONT_BYTES),
        cost_estimate=pl.CostEstimate(
            flops=pairs * 32 * lines * lines * HEAD_DIM,
            bytes_accessed=14 << 20,
            transcendentals=pairs * lines * lines,
        ),
        name="attention_front",
    )(x, *fixed)


def back(up, amino, core, saved, wq, wk, wv, wg, wo, gain):
    xhat, inv, nt, k, v, qt, gate, att, probs = saved
    saved = (in_hbm(xhat), inv, nt, k, v, *(in_hbm(a) for a in (qt, gate, att, probs)))
    members, lines, depth = xhat.shape
    tall, wide = (lines, depth), (depth, lines)
    pairs = members * HEADS
    parcel = shape((depth // 8, MSA + PIECE, depth), BF16)
    return pl.pallas_call(
        back_kernel,
        grid=(members, HEADS // GROUP),
        out_shape=(parcel, parcel),
        in_specs=[whole(up), SMEM, SMEM]
        + [by_member(a) for a in saved[:-1]]
        + [by_group(saved[-1])]
        + [whole(a) for a in (wq, wk, wv, wg, wo, gain)],
        out_specs=[whole(parcel), whole(parcel)],
        scratch_shapes=[
            pltpu.VMEM((members,) + tall, F32),
            pltpu.VMEM(tall, BF16),
            pltpu.VMEM(wide, BF16),
            pltpu.VMEM(tall, F32),
            pltpu.VMEM(tall, F32),
            pltpu.VMEM(tall, F32),
            pltpu.VMEM(wide, BF16),
            pltpu.VMEM(wide, BF16),
            pltpu.VMEM((members, lines // 8, 8, depth), F32),
            pltpu.VMEM((5, depth, depth), F32),
            pltpu.VMEM((8, depth), F32),
        ],
        compiler_params=pltpu.CompilerParams(vmem_limit_bytes=BACK_BYTES),
        cost_estimate=pl.CostEstimate(
            flops=pairs * 64 * lines * lines * HEAD_DIM,
            bytes_accessed=14 << 20,
            transcendentals=0,
        ),
        name="attention_back",
    )(up, amino, core, *saved, wq, wk, wv, wg, wo, gain)


def combine_kernel(core_ref, keep_ref, got_ref, out_ref):
    low = core_ref[0] == 0
    keep, got = keep_ref[...].astype(F32), got_ref[...].astype(F32)
    first = jnp.where(low, keep[:, :MSA], got[:, :MSA])
    second = jnp.where(low, got[:, :MSA], keep[:, :MSA])
    total = keep[:, MSA:] + got[:, MSA:]
    out_ref[...] = jnp.concatenate([first, second, total], 1).astype(BF16)


def combine(core, keep, got):
    chips, _, depth = keep.shape
    return pl.pallas_call(
        combine_kernel,
        out_shape=shape((chips, 2 * MSA + PIECE, depth), BF16),
        in_specs=[SMEM] + specs(2),
        out_specs=specs(1)[0],
        compiler_params=pltpu.CompilerParams(vmem_limit_bytes=24 << 20),
        name="combine",
    )(core, keep, got)


def merge_kernel(parts_ref, out_ref):
    start = parts_ref.shape[1] - PIECE
    total = jnp.sum(parts_ref[...].astype(F32)[:, start:], 0, keepdims=True)
    out_ref[...] = jnp.broadcast_to(total, out_ref.shape).astype(BF16)


def merge(parts, copies):
    return pl.pallas_call(
        merge_kernel,
        out_shape=shape((copies, PIECE, parts.shape[2]), BF16),
        in_specs=specs(1),
        out_specs=specs(1)[0],
        compiler_params=pltpu.CompilerParams(vmem_limit_bytes=24 << 20),
        name="merge",
    )(parts)


def spread_kernel(parts_ref, mats_ref, vecs_ref):
    total = jnp.sum(parts_ref[...].astype(F32), 0)
    mats = jnp.concatenate([total[:, :LANES], total[:16, LANES:]], 0)
    mats_ref[...] = jnp.broadcast_to(mats[None], mats_ref.shape).astype(BF16)
    vecs_ref[...] = total[16:, LANES:]


def spread(parts, copies):
    return pl.pallas_call(
        spread_kernel,
        out_shape=(shape((copies, 40, LANES), BF16), shape((8, LANES), F32)),
        in_specs=specs(1),
        out_specs=specs(2),
        compiler_params=pltpu.CompilerParams(vmem_limit_bytes=24 << 20),
        name="spread",
    )(parts)


def unpack_kernel(factor, core_ref, own_ref, other_ref, vecs_ref, *out_refs):
    low = core_ref[0] == 0
    own, other = own_ref[...].astype(F32), other_ref[...].astype(F32)
    depth = out_refs[0].shape[0]
    for half in range(2):
        lanes = slice(half * LANES, (half + 1) * LANES)
        first = low if half == 0 else jnp.logical_not(low)
        mats = jnp.where(first, own, other) * factor
        for i in range(5):
            out_refs[i][:, lanes] = mats[:, 8 * i : 8 * i + 8].reshape(depth, LANES)
        out_refs[5][:, lanes] = vecs_ref[4 * half : 4 * half + 4, :] * factor


def unpack(core, own, other, vecs, depth, factor):
    return pl.pallas_call(
        functools.partial(unpack_kernel, factor),
        out_shape=(shape((depth, depth), F32),) * 5 + (shape((4, depth), F32),),
        in_specs=[SMEM] + specs(3),
        out_specs=specs(6),
        compiler_params=pltpu.CompilerParams(vmem_limit_bytes=32 << 20),
        name="unpack",
    )(core, own, other, vecs)


def exchange(a, axis, groups=None):
    return lax.all_to_all(
        a, axis, split_axis=0, concat_axis=0, tiled=True, axis_index_groups=groups
    )


def shards(x, up, hom, amino, wq, wk, wv, wg, bg, wo, gain, off):
    _, near, residues, depth = up.shape
    n_dp, n_dap = lax.axis_size("dp"), lax.axis_size("dap")
    lines, members = x.shape[1], x.shape[2]
    chips = n_dap // 2
    partner = [(i, i ^ 1) for i in range(n_dap)]
    same_core = [[2 * i + c for i in range(chips)] for c in range(2)]
    core = (lax.axis_index("dap") % 2).astype(jnp.int32).reshape(1)

    rows = jnp.transpose(up[0].reshape(near, n_dap, members, depth), (1, 2, 0, 3))
    local_up = exchange(rows.reshape(n_dap, members * near, depth), "dap")
    swapped = jnp.transpose(x[0], (1, 0, 2))
    gain, off, bg = gain[None], off[None], bg[None]
    saved = front(swapped, hom, wq, wk, wv, wg, bg, gain, off)
    keep, send = back(local_up, amino, core, saved, wq, wk, wv, wg, wo, gain)

    got = lax.ppermute(send, "dap", partner)
    parts = exchange(combine(core, keep, got), "dap", same_core)
    pieces = exchange(merge(parts, n_dp), "dp")
    mats, vecs = spread(pieces, chips)
    own = exchange(mats, "dap", same_core)
    other = lax.ppermute(own, "dap", partner)
    factor = float((n_dp * lines * residues) ** (-0.5))
    grads = unpack(core, own, other, vecs, depth, factor)

    msa = parts[:, : 2 * MSA].reshape(chips, 2, members, near, depth)
    adjoint = jnp.transpose(msa, (3, 0, 1, 2, 4)).reshape(1, near, residues, depth)
    return (adjoint,) + tuple(grads)


def solution(mesh):
    in_specs = (
        P("dp", None, "dap", None),
        P("dp", "dap", None, None),
        P("dp", None),
        P("dp", "dap"),
    ) + (P(),) * 8
    out_specs = (P("dp", "dap", None, None),) + (P(),) * 6
    return jax.shard_map(shards, mesh=mesh, in_specs=in_specs, out_specs=out_specs, check_vma=False)
```

```python
import functools

import jax
import jax.numpy as jnp
from jax import lax
from jax.experimental import pallas as pl
from jax.experimental.pallas import tpu as pltpu
from jax.sharding import PartitionSpec as P

HEADS = 8
HEAD_DIM = 32
LANES = 128
PIECE = 384
MSA = 256
GROUP = 8
VMEM_BYTES = 60 << 20
FRONT_BYTES = 51 << 20
BACK_BYTES = 50 << 20
EPS = 1e-05
MASKED = 1000000000.0
F32, BF16 = jnp.float32, jnp.bfloat16


def mm(left, right):
    return lax.dot_general(left, right, (((1,), (0,)), ((), ())), preferred_element_type=F32)


def against(left, weight):
    return lax.dot_general(left, weight, (((1,), (1,)), ((), ())), preferred_element_type=F32)


def row_sum(a):
    return jnp.sum(a, 0, keepdims=True)


def front_kernel(
    x_ref,
    *refs,
):
    ins, outs, scratch = refs[:8], refs[8:17], refs[17:]
    xhat_ref, inv_ref, nt_ref, k_ref, v_ref, qt_ref, gate_ref, att_ref, probs_ref = outs
    bufs, (q_s, sems) = scratch[:8], scratch[8:]
    hom_ref, wq_ref, wk_ref, wv_ref, wg_ref, bg_ref, gain_ref, off_ref = bufs
    _, lines, depth = x_ref.shape
    group = probs_ref.shape[1]
    r = pl.program_id(0)
    loads = [pltpu.make_async_copy(ins[i], bufs[i], sems.at[i]) for i in range(8)]
    step = pl.program_id(1)
    lane_head = lax.broadcasted_iota(jnp.int32, (1, depth), 1) // HEAD_DIM

    @pl.when(step == 0)
    def _():
        @pl.when(r == 0)
        def _():
            for load in loads:
                load.start()

        x = x_ref[0].astype(F32)
        centred = x - jnp.mean(x, -1, keepdims=True)
        inv = lax.rsqrt(jnp.mean(centred * centred, -1, keepdims=True) + EPS)
        xhat = centred * inv

        @pl.when(r == 0)
        def _():
            for load in loads:
                load.wait()

        xhat_ref[0] = xhat
        inv_ref[0] = jnp.broadcast_to(inv, (lines, LANES)).T[:8]
        normed = (xhat * gain_ref[...] + off_ref[...]).astype(BF16)
        nt_ref[0] = normed.T
        query = (mm(normed, wq_ref[...]) * HEAD_DIM**-0.5).astype(BF16)
        q_s[...] = query
        qt_ref[0] = query.T
        k_ref[0] = mm(normed, wk_ref[...]).astype(BF16)
        v_ref[0] = mm(normed, wv_ref[...]).astype(BF16)
        gate_ref[0] = jax.nn.sigmoid(mm(normed, wg_ref[...]) + bg_ref[...])
        att_ref[0] = jnp.zeros((lines, depth), F32)

    bias = (hom_ref[...].astype(F32) - 1.0) * MASKED
    for j in range(group):
        own = (lane_head == step * group + j).astype(F32).astype(BF16)
        raised = jnp.exp(against(q_s[...] * own, k_ref[0]) + bias)
        probs = raised * (1.0 / jnp.sum(raised, -1, keepdims=True))
        probs_b = probs.astype(BF16)
        probs_ref[0, j] = probs_b
        att_ref[0] += mm(probs_b, v_ref[0] * own)


def back_kernel(
    up_ref,
    amino_ref,
    core_ref,
    xhat_ref,
    inv_ref,
    nt_ref,
    k_ref,
    v_ref,
    qt_ref,
    gate_ref,
    att_ref,
    probs_ref,
    wq_ref,
    wk_ref,
    wv_ref,
    wg_ref,
    wo_ref,
    gain_ref,
    keep_ref,
    send_ref,
    up_s,
    do_s,
    dot_s,
    prod_s,
    dg_s,
    dq_s,
    dkt_s,
    dvt_s,
    out_s,
    grad_s,
    vec_s,
):
    members, lines, depth = up_s.shape
    group = probs_ref.shape[1]
    r, step = pl.program_id(0), pl.program_id(1)
    last = pl.num_programs(1) - 1
    lane_head = lax.broadcasted_iota(jnp.int32, (1, depth), 1) // HEAD_DIM

    def update():
        return (up_s[r] * amino_ref[0, r].astype(F32)).astype(BF16)

    @pl.when(jnp.logical_and(r == 0, step == 0))
    def _():
        up = up_ref[...].astype(F32)
        for i in range(members):
            up_s[i] = up[:, 8 * i : 8 * i + 8, :].reshape(lines, depth)
        grad_s[...] = jnp.zeros_like(grad_s)
        vec_s[...] = jnp.zeros_like(vec_s)

    @pl.when(step == 0)
    def _():
        dg_s[...] = against(update(), wo_ref[...])
        d_att = (dg_s[...] * gate_ref[0]).astype(BF16)
        do_s[...] = d_att
        dot_s[...] = d_att.T
        prod_s[...] = d_att.astype(F32) * att_ref[0]
        dq_s[...] = jnp.zeros_like(dq_s)

    for j in range(group):
        h = step * group + j
        mask = (lane_head == h).astype(F32)
        own = mask.astype(BF16)
        rows = pl.ds(pl.multiple_of(h * HEAD_DIM, HEAD_DIM), HEAD_DIM)
        probs_b = probs_ref[0, j]
        delta = jnp.sum(prod_s[...] * mask, -1, keepdims=True)
        d_probs = against(do_s[...] * own, v_ref[0])
        d_scores = (probs_b.astype(F32) * (d_probs - delta)).astype(BF16)
        dq_s[...] += mm(d_scores, k_ref[0] * own)
        dkt_s[rows, :] = mm(qt_ref[0, rows, :], d_scores).astype(BF16)
        dvt_s[rows, :] = mm(dot_s[rows, :], probs_b).astype(BF16)

    @pl.when(step == last)
    def _():
        att, gate, d_gated, xhat = att_ref[0], gate_ref[0], dg_s[...], xhat_ref[0]
        d_update = update()
        gated = (gate * att).astype(BF16)
        d_logit = (d_gated * att * gate * (1.0 - gate)).astype(BF16)
        dq = (dq_s[...] * HEAD_DIM**-0.5).astype(BF16)
        dk = dkt_s[...].T
        dv = dvt_s[...].T
        d_normed = (
            against(dq, wq_ref[...])
            + against(dk, wk_ref[...])
            + against(dv, wv_ref[...])
            + against(d_logit, wg_ref[...])
        )
        d_hat = d_normed * gain_ref[...]
        d_branch = inv_ref[0].T[:, :1] * (
            d_hat
            - jnp.mean(d_hat, -1, keepdims=True)
            - xhat * jnp.mean(d_hat * xhat, -1, keepdims=True)
        )
        out_s[r] = (up_s[r] + d_branch).reshape(lines // 8, 8, depth)
        normed_t = nt_ref[0]
        mats = (
            mm(normed_t, dq),
            mm(normed_t, dk),
            mm(normed_t, dv),
            mm(normed_t, d_logit),
            mm(gated.T, d_update),
        )
        vecs = (
            row_sum(d_logit.astype(F32)),
            row_sum(d_update.astype(F32)),
            row_sum(d_normed * xhat),
            row_sum(d_normed),
        )
        for i, g in enumerate(mats):
            grad_s[i] += g
        for i, g in enumerate(vecs):
            vec_s[i : i + 1, :] += g

    @pl.when(jnp.logical_and(r == members - 1, step == last))
    def _():
        low = core_ref[0] == 0
        chips = depth // 8
        rows = jnp.concatenate([out_s[i] for i in range(members)], 1)
        rows = rows.reshape(chips, 2, 8 * members, depth)
        vecs = jnp.concatenate([vec_s[:4, :LANES], vec_s[:4, LANES:]], 0)
        pieces = []
        for half in range(2):
            lanes = slice(half * LANES, (half + 1) * LANES)
            parts = [grad_s[i][:, lanes].reshape(chips, 8, LANES) for i in range(5)]
            parts.append(jnp.broadcast_to(vecs[None], (chips, 8, LANES)))
            pairs = [jnp.concatenate(parts[i : i + 2], 1) for i in (0, 2, 4)]
            pieces.append(jnp.concatenate(pairs, 2))
        zero = jnp.concatenate([rows[:, 0], pieces[0]], 2)
        one = jnp.concatenate([rows[:, 1], pieces[1]], 2)
        keep_ref[...] = jnp.where(low, zero, one).astype(BF16)
        send_ref[...] = jnp.where(low, one, zero).astype(BF16)


def specs(n):
    return [pl.BlockSpec(memory_space=pltpu.VMEM)] * n


SMEM = pl.BlockSpec(memory_space=pltpu.SMEM)
HBM = pl.BlockSpec(memory_space=pltpu.HBM)


def shape(dims, dtype):
    return jax.ShapeDtypeStruct(dims, dtype)


def in_hbm(a):
    return pltpu.with_memory_space_constraint(a, pltpu.HBM)


def whole(a):
    return pl.BlockSpec(a.shape, lambda r, h: (0,) * len(a.shape))


def by_member(a):
    return pl.BlockSpec((1,) + a.shape[1:], lambda r, h: (r,) + (0,) * (len(a.shape) - 1))


def by_group(a):
    return pl.BlockSpec((1, GROUP) + a.shape[2:], lambda r, h: (r, h, 0, 0))


def front(x, hom, wq, wk, wv, wg, bg, gain, off):
    fixed = (hom, wq, wk, wv, wg, bg, gain, off)
    fixed = tuple(in_hbm(a) for a in fixed)
    members, lines, depth = x.shape
    tall, wide = (members, lines, depth), (members, depth, lines)
    pairs = members * HEADS
    outs = (
        shape(tall, F32),
        shape((members, 8, lines), F32),
        shape(wide, BF16),
        shape(tall, BF16),
        shape(tall, BF16),
        shape(wide, BF16),
        shape(tall, F32),
        shape(tall, F32),
        shape((members, HEADS, lines, lines), BF16),
    )
    return pl.pallas_call(
        front_kernel,
        grid=(members, HEADS // GROUP),
        out_shape=outs,
        in_specs=[by_member(x)] + [HBM] * len(fixed),
        out_specs=[by_member(a) for a in outs[:-1]] + [by_group(outs[-1])],
        scratch_shapes=[pltpu.VMEM(a.shape, a.dtype) for a in fixed]
        + [pltpu.VMEM((lines, depth), BF16), pltpu.SemaphoreType.DMA((len(fixed),))],
        compiler_params=pltpu.CompilerParams(vmem_limit_bytes=FRONT_BYTES),
        cost_estimate=pl.CostEstimate(
            flops=pairs * 32 * lines * lines * HEAD_DIM,
            bytes_accessed=14 << 20,
            transcendentals=pairs * lines * lines,
        ),
        name="attention_front",
    )(x, *fixed)


def back(up, amino, core, saved, wq, wk, wv, wg, wo, gain):
    xhat, inv, nt, k, v, qt, gate, att, probs = saved
    saved = (in_hbm(xhat), inv, nt, k, v, *(in_hbm(a) for a in (qt, gate, att, probs)))
    members, lines, depth = xhat.shape
    tall, wide = (lines, depth), (depth, lines)
    pairs = members * HEADS
    parcel = shape((depth // 8, 8 * members, MSA + PIECE), BF16)
    return pl.pallas_call(
        back_kernel,
        grid=(members, HEADS // GROUP),
        out_shape=(parcel, parcel),
        in_specs=[whole(up), SMEM, SMEM]
        + [by_member(a) for a in saved[:-1]]
        + [by_group(saved[-1])]
        + [whole(a) for a in (wq, wk, wv, wg, wo, gain)],
        out_specs=[whole(parcel), whole(parcel)],
        scratch_shapes=[
            pltpu.VMEM((members,) + tall, F32),
            pltpu.VMEM(tall, BF16),
            pltpu.VMEM(wide, BF16),
            pltpu.VMEM(tall, F32),
            pltpu.VMEM(tall, F32),
            pltpu.VMEM(tall, F32),
            pltpu.VMEM(wide, BF16),
            pltpu.VMEM(wide, BF16),
            pltpu.VMEM((members, lines // 8, 8, depth), F32),
            pltpu.VMEM((5, depth, depth), F32),
            pltpu.VMEM((8, depth), F32),
        ],
        compiler_params=pltpu.CompilerParams(vmem_limit_bytes=BACK_BYTES),
        cost_estimate=pl.CostEstimate(
            flops=pairs * 64 * lines * lines * HEAD_DIM,
            bytes_accessed=14 << 20,
            transcendentals=0,
        ),
        name="attention_back",
    )(up, amino, core, *saved, wq, wk, wv, wg, wo, gain)


def combine_kernel(core_ref, keep_ref, got_ref, out_ref):
    low = core_ref[0] == 0
    keep, got = keep_ref[...].astype(F32), got_ref[...].astype(F32)
    first = jnp.where(low, keep[..., :MSA], got[..., :MSA])
    second = jnp.where(low, got[..., :MSA], keep[..., :MSA])
    total = keep[..., MSA:] + got[..., MSA:]
    out_ref[...] = jnp.concatenate([first, second, total], 2).astype(BF16)


def combine(core, keep, got):
    chips, rows, _ = keep.shape
    return pl.pallas_call(
        combine_kernel,
        out_shape=shape((chips, rows, 2 * MSA + PIECE), BF16),
        in_specs=[SMEM] + specs(2),
        out_specs=specs(1)[0],
        compiler_params=pltpu.CompilerParams(vmem_limit_bytes=24 << 20),
        name="combine",
    )(core, keep, got)


def merge_kernel(parts_ref, out_ref):
    total = jnp.sum(parts_ref[:, :, 2 * MSA :].astype(F32), 0, keepdims=True)
    out_ref[...] = jnp.broadcast_to(total, out_ref.shape).astype(BF16)


def merge(parts, copies):
    return pl.pallas_call(
        merge_kernel,
        out_shape=shape((copies, parts.shape[1], PIECE), BF16),
        in_specs=specs(1),
        out_specs=specs(1)[0],
        compiler_params=pltpu.CompilerParams(vmem_limit_bytes=24 << 20),
        name="merge",
    )(parts)


def spread_kernel(parts_ref, mats_ref, vecs_ref):
    total = jnp.sum(parts_ref[...].astype(F32), 0)
    a, b, c = (total[:, i * LANES : (i + 1) * LANES] for i in range(3))
    mats = jnp.concatenate([a, b, c[:8]], 0)
    mats_ref[...] = jnp.broadcast_to(mats[None], mats_ref.shape).astype(BF16)
    vecs_ref[...] = c[8:]


def spread(parts, copies):
    return pl.pallas_call(
        spread_kernel,
        out_shape=(shape((copies, 40, LANES), BF16), shape((8, LANES), F32)),
        in_specs=specs(1),
        out_specs=specs(2),
        compiler_params=pltpu.CompilerParams(vmem_limit_bytes=24 << 20),
        name="spread",
    )(parts)


def unpack_kernel(factor, core_ref, own_ref, other_ref, vecs_ref, *out_refs):
    low = core_ref[0] == 0
    own, other = own_ref[...].astype(F32), other_ref[...].astype(F32)
    depth = out_refs[0].shape[0]
    for half in range(2):
        lanes = slice(half * LANES, (half + 1) * LANES)
        first = low if half == 0 else jnp.logical_not(low)
        mats = jnp.where(first, own, other) * factor
        for i in range(5):
            out_refs[i][:, lanes] = mats[:, 8 * i : 8 * i + 8].reshape(depth, LANES)
        out_refs[5][:, lanes] = vecs_ref[4 * half : 4 * half + 4, :] * factor


def unpack(core, own, other, vecs, depth, factor):
    return pl.pallas_call(
        functools.partial(unpack_kernel, factor),
        out_shape=(shape((depth, depth), F32),) * 5 + (shape((4, depth), F32),),
        in_specs=[SMEM] + specs(3),
        out_specs=specs(6),
        compiler_params=pltpu.CompilerParams(vmem_limit_bytes=32 << 20),
        name="unpack",
    )(core, own, other, vecs)


def exchange(a, axis, groups=None):
    return lax.all_to_all(
        a, axis, split_axis=0, concat_axis=0, tiled=True, axis_index_groups=groups
    )


def shards(x, up, hom, amino, wq, wk, wv, wg, bg, wo, gain, off):
    _, near, residues, depth = up.shape
    n_dp, n_dap = lax.axis_size("dp"), lax.axis_size("dap")
    lines, members = x.shape[1], x.shape[2]
    chips = n_dap // 2
    partner = [(i, i ^ 1) for i in range(n_dap)]
    same_core = [[2 * i + c for i in range(chips)] for c in range(2)]
    core = (lax.axis_index("dap") % 2).astype(jnp.int32).reshape(1)

    rows = jnp.transpose(up[0].reshape(near, n_dap, members, depth), (1, 2, 0, 3))
    local_up = exchange(rows.reshape(n_dap, members * near, depth), "dap")
    swapped = jnp.transpose(x[0], (1, 0, 2))
    gain, off, bg = gain[None], off[None], bg[None]
    saved = front(swapped, hom, wq, wk, wv, wg, bg, gain, off)
    keep, send = back(local_up, amino, core, saved, wq, wk, wv, wg, wo, gain)

    got = lax.ppermute(send, "dap", partner)
    parts = exchange(combine(core, keep, got), "dap", same_core)
    pieces = exchange(merge(parts, n_dp), "dp")
    mats, vecs = spread(pieces, chips)
    own = exchange(mats, "dap", same_core)
    other = lax.ppermute(own, "dap", partner)
    factor = float((n_dp * lines * residues) ** (-0.5))
    grads = unpack(core, own, other, vecs, depth, factor)

    msa = parts[:, :, : 2 * MSA].reshape(chips, members, near, 2, depth)
    adjoint = jnp.transpose(msa, (2, 0, 3, 1, 4)).reshape(1, near, residues, depth)
    return (adjoint,) + tuple(grads)


def solution(mesh):
    in_specs = (
        P("dp", None, "dap", None),
        P("dp", "dap", None, None),
        P("dp", None),
        P("dp", "dap"),
    ) + (P(),) * 8
    out_specs = (P("dp", "dap", None, None),) + (P(),) * 6
    return jax.shard_map(shards, mesh=mesh, in_specs=in_specs, out_specs=out_specs, check_vma=False)
```

```python
import functools

import jax
import jax.numpy as jnp
from jax import lax
from jax.experimental import pallas as pl
from jax.experimental.pallas import tpu as pltpu
from jax.sharding import PartitionSpec as P

HEADS = 8
HEAD_DIM = 32
LANES = 128
PIECE = 24
MSA = 16
GROUP = 8
VMEM_BYTES = 60 << 20
FRONT_BYTES = 51 << 20
BACK_BYTES = 50 << 20
EPS = 1e-05
MASKED = 1000000000.0
F32, BF16 = jnp.float32, jnp.bfloat16


def mm(left, right):
    return lax.dot_general(left, right, (((1,), (0,)), ((), ())), preferred_element_type=F32)


def against(left, weight):
    return lax.dot_general(left, weight, (((1,), (1,)), ((), ())), preferred_element_type=F32)


def row_sum(a):
    return jnp.sum(a, 0, keepdims=True)


def front_kernel(
    x_ref,
    *refs,
):
    ins, outs, scratch = refs[:8], refs[8:17], refs[17:]
    xhat_ref, inv_ref, nt_ref, k_ref, v_ref, qt_ref, gate_ref, att_ref, probs_ref = outs
    bufs, (q_s, sems) = scratch[:8], scratch[8:]
    hom_ref, wq_ref, wk_ref, wv_ref, wg_ref, bg_ref, gain_ref, off_ref = bufs
    _, lines, depth = x_ref.shape
    group = probs_ref.shape[1]
    r = pl.program_id(0)
    loads = [pltpu.make_async_copy(ins[i], bufs[i], sems.at[i]) for i in range(8)]
    step = pl.program_id(1)
    lane_head = lax.broadcasted_iota(jnp.int32, (1, depth), 1) // HEAD_DIM

    @pl.when(step == 0)
    def _():
        @pl.when(r == 0)
        def _():
            for load in loads:
                load.start()

        x = x_ref[0].astype(F32)
        centred = x - jnp.mean(x, -1, keepdims=True)
        inv = lax.rsqrt(jnp.mean(centred * centred, -1, keepdims=True) + EPS)
        xhat = centred * inv

        @pl.when(r == 0)
        def _():
            for load in loads:
                load.wait()

        xhat_ref[0] = xhat
        inv_ref[0] = jnp.broadcast_to(inv, (lines, LANES)).T[:8]
        normed = (xhat * gain_ref[...] + off_ref[...]).astype(BF16)
        nt_ref[0] = normed.T
        query = (mm(normed, wq_ref[...]) * HEAD_DIM**-0.5).astype(BF16)
        q_s[...] = query
        qt_ref[0] = query.T
        k_ref[0] = mm(normed, wk_ref[...]).astype(BF16)
        v_ref[0] = mm(normed, wv_ref[...]).astype(BF16)
        gate_ref[0] = jax.nn.sigmoid(mm(normed, wg_ref[...]) + bg_ref[...])
        att_ref[0] = jnp.zeros((lines, depth), F32)

    bias = (hom_ref[...].astype(F32) - 1.0) * MASKED
    for j in range(group):
        own = (lane_head == step * group + j).astype(F32).astype(BF16)
        raised = jnp.exp(against(q_s[...] * own, k_ref[0]) + bias)
        probs = raised * (1.0 / jnp.sum(raised, -1, keepdims=True))
        probs_b = probs.astype(BF16)
        probs_ref[0, j] = probs_b
        att_ref[0] += mm(probs_b, v_ref[0] * own)


def back_kernel(
    up_ref,
    amino_ref,
    core_ref,
    xhat_ref,
    inv_ref,
    nt_ref,
    k_ref,
    v_ref,
    qt_ref,
    gate_ref,
    att_ref,
    probs_ref,
    wq_ref,
    wk_ref,
    wv_ref,
    wg_ref,
    wo_ref,
    gain_ref,
    keep_ref,
    send_ref,
    up_s,
    do_s,
    dot_s,
    prod_s,
    dg_s,
    dq_s,
    dkt_s,
    dvt_s,
    out_s,
    grad_s,
    vec_s,
):
    members, lines, depth = up_s.shape
    group = probs_ref.shape[1]
    r, step = pl.program_id(0), pl.program_id(1)
    last = pl.num_programs(1) - 1
    lane_head = lax.broadcasted_iota(jnp.int32, (1, depth), 1) // HEAD_DIM

    def update():
        return (up_s[r] * amino_ref[0, r].astype(F32)).astype(BF16)

    @pl.when(jnp.logical_and(r == 0, step == 0))
    def _():
        up = up_ref[...].astype(F32)
        for i in range(members):
            up_s[i] = up[:, 8 * i : 8 * i + 8, :].reshape(lines, depth)
        grad_s[...] = jnp.zeros_like(grad_s)
        vec_s[...] = jnp.zeros_like(vec_s)

    @pl.when(step == 0)
    def _():
        dg_s[...] = against(update(), wo_ref[...])
        d_att = (dg_s[...] * gate_ref[0]).astype(BF16)
        do_s[...] = d_att
        dot_s[...] = d_att.T
        prod_s[...] = d_att.astype(F32) * att_ref[0]
        dq_s[...] = jnp.zeros_like(dq_s)

    for j in range(group):
        h = step * group + j
        mask = (lane_head == h).astype(F32)
        own = mask.astype(BF16)
        rows = pl.ds(pl.multiple_of(h * HEAD_DIM, HEAD_DIM), HEAD_DIM)
        probs_b = probs_ref[0, j]
        delta = jnp.sum(prod_s[...] * mask, -1, keepdims=True)
        d_probs = against(do_s[...] * own, v_ref[0])
        d_scores = (probs_b.astype(F32) * (d_probs - delta)).astype(BF16)
        dq_s[...] += mm(d_scores, k_ref[0] * own)
        dkt_s[rows, :] = mm(qt_ref[0, rows, :], d_scores).astype(BF16)
        dvt_s[rows, :] = mm(dot_s[rows, :], probs_b).astype(BF16)

    @pl.when(step == last)
    def _():
        att, gate, d_gated, xhat = att_ref[0], gate_ref[0], dg_s[...], xhat_ref[0]
        d_update = update()
        gated = (gate * att).astype(BF16)
        d_logit = (d_gated * att * gate * (1.0 - gate)).astype(BF16)
        dq = (dq_s[...] * HEAD_DIM**-0.5).astype(BF16)
        dk = dkt_s[...].T
        dv = dvt_s[...].T
        d_normed = (
            against(dq, wq_ref[...])
            + against(dk, wk_ref[...])
            + against(dv, wv_ref[...])
            + against(d_logit, wg_ref[...])
        )
        d_hat = d_normed * gain_ref[...]
        d_branch = inv_ref[0].T[:, :1] * (
            d_hat
            - jnp.mean(d_hat, -1, keepdims=True)
            - xhat * jnp.mean(d_hat * xhat, -1, keepdims=True)
        )
        out_s[r] = (up_s[r] + d_branch).reshape(lines // 8, 8, depth)
        normed_t = nt_ref[0]
        mats = (
            mm(normed_t, dq),
            mm(normed_t, dk),
            mm(normed_t, dv),
            mm(normed_t, d_logit),
            mm(gated.T, d_update),
        )
        vecs = (
            row_sum(d_logit.astype(F32)),
            row_sum(d_update.astype(F32)),
            row_sum(d_normed * xhat),
            row_sum(d_normed),
        )
        for i, g in enumerate(mats):
            grad_s[i] += g
        for i, g in enumerate(vecs):
            vec_s[i : i + 1, :] += g

    @pl.when(jnp.logical_and(r == members - 1, step == last))
    def _():
        low = core_ref[0] == 0
        chips = depth // 8
        rows = jnp.concatenate([out_s[i] for i in range(members)], 1)
        rows = rows.reshape(chips, 2, MSA, depth)
        vecs = jnp.concatenate([vec_s[:4, :LANES], vec_s[:4, LANES:]], 0)
        pieces = []
        for half in range(2):
            lanes = slice(half * LANES, (half + 1) * LANES)
            parts = [grad_s[i][:, lanes].reshape(chips, 8, LANES) for i in range(5)]
            parts.append(jnp.broadcast_to(vecs[None], (chips, 8, LANES)))
            left, right = jnp.concatenate(parts[:3], 1), jnp.concatenate(parts[3:], 1)
            pieces.append(jnp.concatenate([left, right], 2))
        zero = jnp.concatenate([rows[:, 0], pieces[0]], 1)
        one = jnp.concatenate([rows[:, 1], pieces[1]], 1)
        keep_ref[...] = jnp.where(low, zero, one).astype(BF16)
        send_ref[...] = jnp.where(low, one, zero).astype(BF16)


def specs(n):
    return [pl.BlockSpec(memory_space=pltpu.VMEM)] * n


SMEM = pl.BlockSpec(memory_space=pltpu.SMEM)
HBM = pl.BlockSpec(memory_space=pltpu.HBM)


def shape(dims, dtype):
    return jax.ShapeDtypeStruct(dims, dtype)


def in_hbm(a):
    return pltpu.with_memory_space_constraint(a, pltpu.HBM)


def whole(a):
    return pl.BlockSpec(a.shape, lambda r, h: (0,) * len(a.shape))


def by_member(a):
    return pl.BlockSpec((1,) + a.shape[1:], lambda r, h: (r,) + (0,) * (len(a.shape) - 1))


def by_group(a):
    return pl.BlockSpec((1, GROUP) + a.shape[2:], lambda r, h: (r, h, 0, 0))


def front(x, hom, wq, wk, wv, wg, bg, gain, off):
    fixed = (hom, wq, wk, wv, wg, bg, gain, off)
    fixed = tuple(in_hbm(a) for a in fixed)
    members, lines, depth = x.shape
    tall, wide = (members, lines, depth), (members, depth, lines)
    pairs = members * HEADS
    outs = (
        shape(tall, F32),
        shape((members, 8, lines), F32),
        shape(wide, BF16),
        shape(tall, BF16),
        shape(tall, BF16),
        shape(wide, BF16),
        shape(tall, F32),
        shape(tall, F32),
        shape((members, HEADS, lines, lines), BF16),
    )
    return pl.pallas_call(
        front_kernel,
        grid=(members, HEADS // GROUP),
        out_shape=outs,
        in_specs=[by_member(x)] + [HBM] * len(fixed),
        out_specs=[by_member(a) for a in outs[:-1]] + [by_group(outs[-1])],
        scratch_shapes=[pltpu.VMEM(a.shape, a.dtype) for a in fixed]
        + [pltpu.VMEM((lines, depth), BF16), pltpu.SemaphoreType.DMA((len(fixed),))],
        compiler_params=pltpu.CompilerParams(vmem_limit_bytes=FRONT_BYTES),
        cost_estimate=pl.CostEstimate(
            flops=pairs * 32 * lines * lines * HEAD_DIM,
            bytes_accessed=14 << 20,
            transcendentals=pairs * lines * lines,
        ),
        name="attention_front",
    )(x, *fixed)


def back(up, amino, core, saved, wq, wk, wv, wg, wo, gain):
    xhat, inv, nt, k, v, qt, gate, att, probs = saved
    saved = (in_hbm(xhat), inv, nt, k, v, *(in_hbm(a) for a in (qt, gate, att, probs)))
    members, lines, depth = xhat.shape
    tall, wide = (lines, depth), (depth, lines)
    pairs = members * HEADS
    parcel = shape((depth // 8, MSA + PIECE, depth), BF16)
    return pl.pallas_call(
        back_kernel,
        grid=(members, HEADS // GROUP),
        out_shape=(parcel, parcel),
        in_specs=[whole(up), SMEM, SMEM]
        + [by_member(a) for a in saved[:-1]]
        + [by_group(saved[-1])]
        + [whole(a) for a in (wq, wk, wv, wg, wo, gain)],
        out_specs=[whole(parcel), whole(parcel)],
        scratch_shapes=[
            pltpu.VMEM((members,) + tall, F32),
            pltpu.VMEM(tall, BF16),
            pltpu.VMEM(wide, BF16),
            pltpu.VMEM(tall, F32),
            pltpu.VMEM(tall, F32),
            pltpu.VMEM(tall, F32),
            pltpu.VMEM(wide, BF16),
            pltpu.VMEM(wide, BF16),
            pltpu.VMEM((members, lines // 8, 8, depth), F32),
            pltpu.VMEM((5, depth, depth), F32),
            pltpu.VMEM((8, depth), F32),
        ],
        compiler_params=pltpu.CompilerParams(vmem_limit_bytes=BACK_BYTES),
        cost_estimate=pl.CostEstimate(
            flops=pairs * 64 * lines * lines * HEAD_DIM,
            bytes_accessed=14 << 20,
            transcendentals=0,
        ),
        name="attention_back",
    )(up, amino, core, *saved, wq, wk, wv, wg, wo, gain)


def combine_kernel(core_ref, keep_ref, got_ref, out_ref):
    low = core_ref[0] == 0
    keep, got = keep_ref[...].astype(F32), got_ref[...].astype(F32)
    first = jnp.where(low, keep[:, :MSA], got[:, :MSA])
    second = jnp.where(low, got[:, :MSA], keep[:, :MSA])
    total = keep[:, MSA:] + got[:, MSA:]
    out_ref[...] = jnp.concatenate([first, second, total], 1).astype(BF16)


def combine(core, keep, got):
    chips, _, depth = keep.shape
    return pl.pallas_call(
        combine_kernel,
        out_shape=shape((chips, 2 * MSA + PIECE, depth), BF16),
        in_specs=[SMEM] + specs(2),
        out_specs=specs(1)[0],
        compiler_params=pltpu.CompilerParams(vmem_limit_bytes=24 << 20),
        name="combine",
    )(core, keep, got)


def merge_kernel(parts_ref, out_ref):
    start = parts_ref.shape[1] - PIECE
    total = jnp.sum(parts_ref[...].astype(F32)[:, start:], 0, keepdims=True)
    out_ref[...] = jnp.broadcast_to(total, out_ref.shape).astype(BF16)


def merge(parts, copies):
    return pl.pallas_call(
        merge_kernel,
        out_shape=shape((copies, PIECE, parts.shape[2]), BF16),
        in_specs=specs(1),
        out_specs=specs(1)[0],
        compiler_params=pltpu.CompilerParams(vmem_limit_bytes=24 << 20),
        name="merge",
    )(parts)


def spread_kernel(parts_ref, after_ref, mats_ref, vecs_ref):
    total = jnp.sum(parts_ref[...].astype(F32), 0)
    mats = jnp.concatenate([total[:, :LANES], total[:16, LANES:]], 0)
    mats_ref[...] = jnp.broadcast_to(mats[None], mats_ref.shape).astype(BF16)
    vecs_ref[...] = total[16:, LANES:]


def spread(parts, after, copies):
    return pl.pallas_call(
        spread_kernel,
        out_shape=(shape((copies, 40, LANES), BF16), shape((8, LANES), F32)),
        in_specs=specs(1) + [pl.BlockSpec(memory_space=pl.ANY)],
        out_specs=specs(2),
        compiler_params=pltpu.CompilerParams(vmem_limit_bytes=24 << 20),
        name="spread",
    )(parts, after)


def unpack_kernel(factor, core_ref, own_ref, other_ref, vecs_ref, *out_refs):
    low = core_ref[0] == 0
    own, other = own_ref[...].astype(F32), other_ref[...].astype(F32)
    depth = out_refs[0].shape[0]
    for half in range(2):
        lanes = slice(half * LANES, (half + 1) * LANES)
        first = low if half == 0 else jnp.logical_not(low)
        mats = jnp.where(first, own, other) * factor
        for i in range(5):
            out_refs[i][:, lanes] = mats[:, 8 * i : 8 * i + 8].reshape(depth, LANES)
        out_refs[5][:, lanes] = vecs_ref[4 * half : 4 * half + 4, :] * factor


def unpack(core, own, other, vecs, depth, factor):
    return pl.pallas_call(
        functools.partial(unpack_kernel, factor),
        out_shape=(shape((depth, depth), F32),) * 5 + (shape((4, depth), F32),),
        in_specs=[SMEM] + specs(3),
        out_specs=specs(6),
        compiler_params=pltpu.CompilerParams(vmem_limit_bytes=32 << 20),
        name="unpack",
    )(core, own, other, vecs)


def exchange(a, axis, groups=None):
    return lax.all_to_all(
        a, axis, split_axis=0, concat_axis=0, tiled=True, axis_index_groups=groups
    )


def shards(x, up, hom, amino, wq, wk, wv, wg, bg, wo, gain, off):
    _, near, residues, depth = up.shape
    n_dp, n_dap = lax.axis_size("dp"), lax.axis_size("dap")
    lines, members = x.shape[1], x.shape[2]
    chips = n_dap // 2
    partner = [(i, i ^ 1) for i in range(n_dap)]
    same_core = [[2 * i + c for i in range(chips)] for c in range(2)]
    core = (lax.axis_index("dap") % 2).astype(jnp.int32).reshape(1)

    rows = jnp.transpose(up[0].reshape(near, n_dap, members, depth), (1, 2, 0, 3))
    local_up = exchange(rows.reshape(n_dap, members * near, depth), "dap")
    swapped = jnp.transpose(x[0], (1, 0, 2))
    gain, off, bg = gain[None], off[None], bg[None]
    saved = front(swapped, hom, wq, wk, wv, wg, bg, gain, off)
    keep, send = back(local_up, amino, core, saved, wq, wk, wv, wg, wo, gain)

    got = lax.ppermute(send, "dap", partner)
    parts = exchange(combine(core, keep, got), "dap", same_core)
    pieces = exchange(merge(parts, n_dp), "dp")
    msa = parts[:, : 2 * MSA].reshape(chips, 2, members, near, depth)
    adjoint = jnp.transpose(msa, (3, 0, 1, 2, 4)).reshape(1, near, residues, depth)
    mats, vecs = spread(pieces, adjoint, chips)
    own = exchange(mats, "dap", same_core)
    other = lax.ppermute(own, "dap", partner)
    factor = float((n_dp * lines * residues) ** (-0.5))
    grads = unpack(core, own, other, vecs, depth, factor)

    return (adjoint,) + tuple(grads)


def solution(mesh):
    in_specs = (
        P("dp", None, "dap", None),
        P("dp", "dap", None, None),
        P("dp", None),
        P("dp", "dap"),
    ) + (P(),) * 8
    out_specs = (P("dp", "dap", None, None),) + (P(),) * 6
    return jax.shard_map(shards, mesh=mesh, in_specs=in_specs, out_specs=out_specs, check_vma=False)
```
